128 devices in a mesh: dp: 8 (over y, z_lo), mp: 16 (over z_hi, x, core).
Axes of the slice: x: 4, y: 4, z: 4 (z_hi: 2, z_lo: 2; z = z_hi * 2 + z_lo), core: 2. Of those that a mesh axis runs over, the one named last changes fastest.
Arguments:
- attn_values: bfloat16 [2048, 4096], P('dp', 'mp'), may hold values from -6 to 6
- out_proj: bfloat16 [4096, 4608], P('mp'), may hold values from -0.1875 to 0.1875
- post_gain: float32 [4608], replicated, may hold values from 0.1 to 1.9
- residual: bfloat16 [2048, 4608], P(('dp', 'mp')), may hold values from -8.5 to 8.5
- sae_weight: bfloat16 [4608, 32768], P(None, 'mp'), may hold values from -0.09375 to 0.09375
- enc_bias: float32 [32768], P('mp'), may hold values from -3 to 3
- dec_bias: float32 [4608], replicated, may hold values from -3 to 3
Outputs:
- stream: bfloat16 [2048, 4608], P(('dp', 'mp'))
- weight_grad: float32 [4608, 32768], P('dp', 'mp')
- enc_bias_grad: float32 [32768], P('mp')
- dec_bias_grad: float32 [4608], replicated
The draws below stay inside these ranges and needn't reach their ends.
All inputs are finite; a program needn't handle non-finite values.
Results may differ from the reference program's by a relative error of at most 0.0095.
Values may be sent and summed in bfloat16 or wider, within the bound.
A program may use at most 192 MiB of HBM per device.

```python
import math
import jax
import jax.numpy as jnp
from jax import lax

D = 4608
HEADS = 32
HEAD_DIM = 128
LAT = 32768
TOK_DEV = 256
TOKENS = 2048
N_DP = 8


def draw_out_proj(key, part):
    key = jax.random.fold_in(key, 11)
    base_key, column_key = jax.random.split(key)
    column_scale = jnp.exp(jax.random.uniform(column_key, (D,), minval=math.log(0.3), maxval=math.log(3.0)))
    base = jnp.clip(jax.random.normal(base_key, (HEADS * HEAD_DIM, D)), -4.0, 4.0)
    limit = 12.0 / math.sqrt(HEADS * HEAD_DIM)
    scaled = jnp.clip(base * column_scale / math.sqrt(HEADS * HEAD_DIM), -limit, limit)
    return scaled.astype(jnp.bfloat16)


def draw_residual(key, part):
    key = jax.random.fold_in(key, 23)
    noise_key, common_key = jax.random.split(key)
    position = jnp.arange(TOKENS, dtype=jnp.float32) / TOKENS
    common = jnp.clip(jax.random.normal(common_key, (D,)), -3.0, 3.0)
    noise = jnp.clip(jax.random.normal(noise_key, (TOKENS, D)), -4.0, 4.0)
    ramp = 0.5 + position
    values = noise + 0.5 * ramp[:, None] * common[None, :]
    return jnp.clip(values, -8.5, 8.5).astype(jnp.bfloat16)


def block_levels(rng, extent, cuts, smallest, top_value):
    loudness, own = 1.0, jax.random.fold_in(rng, 6)
    for dim, parts in cuts:
        draws = jnp.exp(jax.random.uniform(jax.random.fold_in(own, dim), (parts,), jnp.float32, smallest / len(cuts), top_value / len(cuts)))
        loudness = loudness * jnp.repeat(draws, extent[dim] // parts).reshape([-1 if axis == dim else 1 for axis in range(len(extent))])
    return loudness


def scatter_about(own_key, dims, width, most, pieces=(), kind=jnp.bfloat16):
    factor_of = block_levels(own_key, dims, pieces, -0.22, 0.18) if pieces else 1.0
    result = jax.random.normal(own_key, dims, jnp.float32) * width * factor_of
    return jnp.minimum(jnp.maximum(result, -most), most).astype(kind)


def setup_inputs(seed: int = 0) -> dict:
    key_list = jax.random.split(jax.random.key(seed), 8)
    attn_values = scatter_about(key_list[0], (TOKENS, HEADS * HEAD_DIM), 1.0, 6.0, ((0, 8), (1, 16)))
    out_proj = draw_out_proj(jax.random.fold_in(key_list[7], 71), 0)
    post_gain = jnp.clip(1.0 + 0.18 * jax.random.normal(key_list[2], (D,), jnp.float32), 0.1, 1.9)
    residual = draw_residual(jax.random.fold_in(key_list[7], 71), 0)
    sae_weight = scatter_about(key_list[4], (D, LAT), D ** -0.5, 0.09375, ((1, 16),))
    enc_bias = scatter_about(key_list[5], (LAT,), 0.5, 3.0, ((0, 16),), jnp.float32)
    dec_bias = scatter_about(key_list[6], (D,), 0.5, 3.0, (), jnp.float32)
    return {"attn_values": attn_values, "out_proj": out_proj, "post_gain": post_gain, "residual": residual, "sae_weight": sae_weight, "enc_bias": enc_bias, "dec_bias": dec_bias}


SPARSITY = 0.5
LAST_CONTRACT = (((1,), (1,)), ((), ()))
FIRST_CONTRACT = (((0,), (0,)), ((), ()))

def rms_scale(values, post_gain):
    mean_sq = lax.optimization_barrier(jnp.mean(values * values, axis=-1, keepdims=True))
    return values * lax.rsqrt(mean_sq + 1e-06) * post_gain

def reference(attn_values, out_proj, post_gain, residual, sae_weight, enc_bias, dec_bias):
    attn_out = jnp.dot(attn_values, out_proj, preferred_element_type=jnp.float32)
    stream = (residual.astype(jnp.float32) + rms_scale(attn_out, post_gain)).astype(jnp.bfloat16)
    centered = (stream.astype(jnp.float32) - dec_bias).astype(jnp.bfloat16)
    preact = jnp.dot(centered, sae_weight, preferred_element_type=jnp.float32) + enc_bias
    positive = jnp.maximum(preact, 0.0)
    latent = (positive * positive).astype(jnp.bfloat16)
    recon = lax.dot_general(latent, sae_weight, LAST_CONTRACT, preferred_element_type=jnp.float32) + dec_bias
    loss_scale = 1.0 / math.sqrt(TOKENS)
    err_grad = ((recon - stream.astype(jnp.float32)) * loss_scale).astype(jnp.bfloat16)
    lat_grad = jnp.dot(err_grad, sae_weight, preferred_element_type=jnp.float32) + SPARSITY * loss_scale
    pre_grad = (lat_grad * (2.0 * positive)).astype(jnp.bfloat16)
    weight_grad = jnp.zeros((D, LAT), jnp.float32)
    for shard in range(N_DP):
        first = shard * TOK_DEV
        part = lax.dot_general(centered[first:first + TOK_DEV], pre_grad[first:first + TOK_DEV], FIRST_CONTRACT, preferred_element_type=jnp.float32)
        part = part + lax.dot_general(err_grad[first:first + TOK_DEV], latent[first:first + TOK_DEV], FIRST_CONTRACT, preferred_element_type=jnp.float32)
        weight_grad = weight_grad + lax.optimization_barrier(part.astype(jnp.bfloat16)).astype(jnp.float32)
    enc_bias_grad = lax.optimization_barrier(jnp.sum(pre_grad.astype(jnp.float32), axis=0))
    projected = jnp.dot(sae_weight.astype(jnp.float32), enc_bias_grad, precision=lax.Precision.HIGHEST)
    dec_bias_grad = lax.optimization_barrier(jnp.sum(err_grad.astype(jnp.float32), axis=0)) - projected
    return (stream, weight_grad, enc_bias_grad, dec_bias_grad)
```

```python
import math

import jax
import jax.numpy as jnp
from jax import lax
from jax.experimental import pallas as pl
from jax.experimental.pallas import tpu as pltpu
from jax.sharding import PartitionSpec as P

SPARSITY = 0.5
D = 4608
LAT = 1024
HALF = D // 2
ROWS = 16
TOK = 512
QROWS = D // 4
SUB = QROWS // 3
OWN = QROWS // 2
TOKENS = 2048
SCALE = 1.0 / math.sqrt(TOKENS)
F32 = jnp.float32
BF16 = jnp.bfloat16
H0 = pl.ds(0, HALF)
H1 = pl.ds(HALF, HALF)
LAST = (((1,), (1,)), ((), ()))
FIRST = (((0,), (0,)), ((), ()))


def kernel(
    attn, oproj, gain, resid, w_hbm, ebias, dbias,
    stream, wgrad, enc_out, dec_out,
    w_v, cen, err, pos, lat, pre,
    rsend, rown, rrecv, p1recv, p1r2,
    rz, rx, s2a, s2b, r2a, r2b,
    ysend, yrecv, zsend, zrecv, tmp,
    es3, esr, ezr, dcore, dx_r, dz_r, dy_r,
    w_sem, p1_s, p1_r, p2_s, p2_r, ag_s, ag_r, rc_s, rc_r, r1_s, r1_r, r2_s, r2_r,
    y_s, y_r, z_s, z_r, b_s, b_r,
):
    dp, mp = lax.axis_index("dp"), lax.axis_index("mp")
    y, zl = dp // 2, dp % 2
    zh, x, c = mp // 8, (mp // 2) % 4, mp % 2
    z = zh * 2 + zl

    def dev(x_, y_, z_, c_):
        return (y_ * 2 + z_ % 2, (z_ // 2) * 8 + x_ * 2 + c_)

    core = dev(x, y, z, 1 - c)

    def xpeer(k):
        return dev((x + k) % 4, y, z, c)

    def zpeer(k):
        return dev(x, y, (z + k) % 4, c)

    def ypeer(k):
        return dev(x, (y + k) % 4, z, c)

    zpart = dev(x, y, zh * 2 + 1 - zl, c)

    def far(j):
        return dev((x + j % 4) % 4, y, ((zh + j // 4) % 2) * 2 + zl, c)

    def remote(src, dst, ssem, rsem, to):
        return pltpu.make_async_remote_copy(
            src_ref=src, dst_ref=dst, send_sem=ssem, recv_sem=rsem,
            device_id=to, device_id_type=pl.DeviceIdType.MESH,
        )

    w_copy = pltpu.make_async_copy(
        w_hbm.at[:, pl.ds(pl.multiple_of(zl * LAT, LAT), LAT)], w_v, w_sem
    )
    w_copy.start()

    barrier = pltpu.get_barrier_semaphore()
    partners = [core]
    for k in (1, 2, 3):
        partners += [xpeer(k), zpeer(k), ypeer(k), far(4 + k)]
    for to in partners:
        pl.semaphore_signal(barrier, inc=1, device_id=to, device_id_type=pl.DeviceIdType.MESH)
    pl.semaphore_wait(barrier, len(partners))

    def proj(which):
        return attn[:, :, pl.ds(which, 1)].reshape(128, 256)

    def peer_proj(j, carry):
        cols = pl.ds(pl.multiple_of(j * 512, 512), 512)
        part = jnp.dot(proj(1 - c), oproj[:, cols], preferred_element_type=F32)
        rsend[pl.ds(0, 2), :, :, cols] = part.astype(BF16).reshape(2, 4, ROWS, 512)
        return carry

    lax.fori_loop(0, 9, peer_proj, 0)
    p1 = remote(rsend.at[pl.ds(0, 2)], p1recv, p1_s, p1_r, core)
    p1.start()

    def own_proj(j, carry):
        cols = pl.ds(pl.multiple_of(j * 512, 512), 512)
        part = jnp.dot(proj(c), oproj[:, cols], preferred_element_type=F32)
        rown[pl.ds(0, 2), :, :, cols] = part.reshape(2, 4, ROWS, 512)
        return carry

    lax.fori_loop(0, 9, own_proj, 0)
    p1.wait()

    def add_proj(j, carry):
        total = rown[j // 4, j % 4] + p1recv[j // 4, j % 4].astype(F32)
        rown[j // 4, j % 4] = total
        p1recv[j // 4, j % 4] = total.astype(BF16)
        return carry

    lax.fori_loop(0, 8, add_proj, 0)
    p2 = [
        remote(
            p1recv.at[(zh + j // 4) % 2, (x + j % 4) % 4], p1r2.at[j - 1],
            p2_s.at[j - 1], p2_r.at[j - 1], far(j),
        )
        for j in range(1, 8)
    ]
    for copy in p2:
        copy.start()
    for copy in p2:
        copy.wait()
    attn_out = rown[zh, x]
    for j in range(7):
        attn_out = attn_out + p1r2[j].astype(F32)
    mean_sq = jnp.mean(attn_out * attn_out, axis=-1, keepdims=True)
    normed = attn_out * lax.rsqrt(mean_sq + 1e-06) * gain[...]
    own_stream = (resid[...].astype(F32) + normed).astype(BF16)
    stream[...] = own_stream
    cen[c, z, x] = (own_stream.astype(F32) - dbias[...]).astype(BF16)

    def gather(buf, phase):
        s_sem, r_sem = ag_s.at[phase], ag_r.at[phase]
        own_z = buf.at[c, z, :, :, H0]
        own_x = buf.at[c, :, x, :, H1]
        first = []
        for k in (1, 2, 3):
            mine = buf.at[c, z, x, :, H0]
            first.append(remote(mine, mine, s_sem.at[k], r_sem.at[k], xpeer(k)))
            mine = buf.at[c, z, x, :, H1]
            first.append(remote(mine, mine, s_sem.at[3 + k], r_sem.at[3 + k], zpeer(k)))
        for copy in first:
            copy.start()
        for copy in first:
            copy.wait()
        second = []
        for k in (1, 2, 3):
            second.append(remote(own_z, own_z, s_sem.at[6 + k], r_sem.at[6 + k], zpeer(k)))
            second.append(remote(own_x, own_x, s_sem.at[9 + k], r_sem.at[9 + k], xpeer(k)))
        for copy in second:
            copy.start()
        third = [
            remote(own_z, own_z, s_sem.at[13], r_sem.at[13], core),
            remote(own_x, own_x, s_sem.at[14], r_sem.at[14], core),
        ]
        for copy in third:
            copy.start()
        for k in (1, 2, 3):
            second[2 * k - 2].wait()
            came = buf.at[c, (z + 4 - k) % 4, :, :, H0]
            third.append(remote(came, came, s_sem.at[14 + k], r_sem.at[14 + k], core))
            third[-1].start()
            second[2 * k - 1].wait()
            came = buf.at[c, :, (x + 4 - k) % 4, :, H1]
            third.append(remote(came, came, s_sem.at[17 + k], r_sem.at[17 + k], core))
            third[-1].start()
        for copy in third:
            copy.wait()

    gather(cen, 0)
    w_copy.wait()

    def encode(n, carry):
        cols = pl.ds(pl.multiple_of(n * 256, 256), 256)
        act = jnp.dot(cen[...].reshape(TOK, D), w_v[:, cols], preferred_element_type=F32)
        act = jnp.maximum(act + ebias[pl.ds(zl, 1), cols], 0.0)
        pos[:, cols] = act
        lat[:, cols] = (act * act).astype(BF16)
        return carry

    lax.fori_loop(0, 4, encode, 0)

    def decode(which, j):
        cols = pl.ds(pl.multiple_of(j * 256, 256), 256)
        rows = lat[pl.ds(pl.multiple_of(which * 256, 256), 256), :]
        part = lax.dot_general(rows, w_v[cols, :], LAST, preferred_element_type=F32)
        return cols, part.reshape(4, 4, ROWS, 256)

    def peer_decode(j, carry):
        cols, part = decode(1 - c, j)
        rsend[:, :, :, cols] = part.astype(BF16)
        return carry

    def own_decode(j, carry):
        cols, part = decode(c, j)
        rown[:, :, :, cols] = part
        return carry

    rc = []
    for h, cols in enumerate((H0, H1)):
        lax.fori_loop(9 * h, 9 * h + 9, peer_decode, 0)
        rc.append(
            remote(rsend.at[:, :, :, cols], rrecv.at[:, :, :, cols], rc_s.at[h], rc_r.at[h], core)
        )
        rc[-1].start()
    r1 = []
    for h, cols in enumerate((H0, H1)):
        lax.fori_loop(9 * h, 9 * h + 9, own_decode, 0)
        rc[h].wait()

        def add_decode(j, carry, cols=cols):
            total = rown[j // 4, j % 4, :, cols] + rrecv[j // 4, j % 4, :, cols].astype(F32)
            rown[j // 4, j % 4, :, cols] = total
            rrecv[j // 4, j % 4, :, cols] = total.astype(BF16)
            return carry

        lax.fori_loop(0, 16, add_decode, 0)
        for k in (1, 2, 3):
            if h == 0:
                src, dst, to = rrecv.at[(z + k) % 4, :, :, H0], rz.at[k - 1], zpeer(k)
            else:
                src, dst, to = rrecv.at[:, (x + k) % 4, :, H1], rx.at[k - 1], xpeer(k)
            i = 3 * h + k - 1
            r1.append(remote(src, dst, r1_s.at[i], r1_r.at[i], to))
            r1[-1].start()
    r2 = []
    for h in (0, 1):
        for k in (1, 2, 3):
            r1[3 * h + k - 1].wait()
        for i in range(4):
            if h == 0:
                total = rown[z, i, :, H0]
                for k in range(3):
                    total = total + rz[k, i].astype(F32)
                rown[z, i, :, H0] = total
                s2a[i] = total.astype(BF16)
            else:
                total = rown[i, x, :, H1]
                for k in range(3):
                    total = total + rx[k, i].astype(F32)
                rown[i, x, :, H1] = total
                s2b[i] = total.astype(BF16)
        for k in (1, 2, 3):
            if h == 0:
                src, dst, to = s2a.at[(x + k) % 4], r2a.at[k - 1], xpeer(k)
            else:
                src, dst, to = s2b.at[(z + k) % 4], r2b.at[k - 1], zpeer(k)
            i = 3 * h + k - 1
            r2.append(remote(src, dst, r2_s.at[i], r2_r.at[i], to))
            r2[-1].start()
    err_sums = []
    for h, cols in enumerate((H0, H1)):
        for k in (1, 2, 3):
            r2[3 * h + k - 1].wait()
        total = rown[z, x, :, cols]
        for k in range(3):
            total = total + (r2a, r2b)[h][k].astype(F32)
        grad = (total + dbias[:, cols] - stream[:, cols].astype(F32)) * SCALE
        grad = grad.astype(BF16)
        err[c, z, x, :, cols] = grad
        dcore[pl.ds(c, 1), cols] = jnp.sum(grad.astype(F32), axis=0, keepdims=True)

    gather(err, 1)

    def back(n, carry):
        cols = pl.ds(pl.multiple_of(n * 256, 256), 256)
        grad = jnp.dot(err[...].reshape(TOK, D), w_v[:, cols], preferred_element_type=F32)
        grad = ((grad + SPARSITY * SCALE) * (2.0 * pos[:, cols])).astype(BF16)
        pre[:, cols] = grad
        esr[pl.ds(y, 1), cols] = jnp.sum(grad.astype(F32), axis=0, keepdims=True)
        return carry

    lax.fori_loop(0, 4, back, 0)

    def partial(q, sub, way):
        at = pl.ds(pl.multiple_of(q * QROWS + sub * SUB, SUB), SUB)
        cols = pl.ds(pl.multiple_of(way * 512, 512), 512)
        part = lax.dot_general(
            cen[:, :, :, :, at].reshape(TOK, SUB), pre[:, cols], FIRST, preferred_element_type=F32
        )
        return part + lax.dot_general(
            err[:, :, :, :, at].reshape(TOK, SUB), lat[:, cols], FIRST, preferred_element_type=F32
        )

    def sub_of(k):
        return 1 + (k - 1) * (2 * zl - 1)

    def ring(step, i):
        way = i % 2
        src = ysend.at[i] if step == 0 else yrecv.at[step - 1, i]
        to = dev(x, (y + 1 + 2 * way) % 4, z, c)
        return remote(src, yrecv.at[step, i], y_s.at[step, i], y_r.at[step, i], to)

    def owner(step, way):
        return (y + 7 - step + way * (2 * step + 2)) % 4

    def ring_step(step):
        def body(i, carry):
            k, way = i // 2, i % 2
            part = partial(owner(step, way), sub_of(k), way)
            if step == 0:
                ysend[i] = part.astype(BF16)
            else:
                ring(step - 1, i).wait_recv()
                yrecv[step - 1, i] = (yrecv[step - 1, i].astype(F32) + part).astype(BF16)
            ring(step, i).start()
            return carry

        lax.fori_loop(0, 6, body, 0)

    def b_copy(src, dst, i, to):
        return remote(src, dst, b_s.at[i], b_r.at[i], to)

    ring_step(0)

    own_sum = esr[pl.ds(y, 1), :]
    high = own_sum.astype(BF16)
    rest = own_sum - high.astype(F32)
    mid = rest.astype(BF16)
    low = (rest - mid.astype(F32)).astype(BF16)
    es3[...] = jnp.concatenate([high, mid, low, jnp.zeros((13, LAT), BF16)], axis=0)

    def project(j, carry):
        cols = pl.ds(pl.multiple_of(j * 512, 512), 512)
        part = lax.dot_general(es3[...], w_v[cols, :], LAST, preferred_element_type=F32)
        dcore[pl.ds(c, 1), cols] = dcore[pl.ds(c, 1), cols] - jnp.sum(part, axis=0, keepdims=True)
        return carry

    lax.fori_loop(0, 9, project, 0)
    bias = []
    mine = esr.at[pl.ds(y, 1)]
    for k in (1, 2, 3):
        bias.append(b_copy(mine, mine, k - 1, ypeer(k)))
    mine = dcore.at[pl.ds(c, 1)]
    bias.append(b_copy(mine, mine, 3, core))
    for copy in bias:
        copy.start()

    def dec_stage(slots, value, me, first, peer):
        slots[pl.ds(me, 1), :] = value
        mine = slots.at[pl.ds(me, 1)]
        out = [b_copy(mine, mine, first + k, peer(k + 1)) for k in range(3)]
        for copy in out:
            copy.start()
        return out

    def ordered(slots, count):
        total = slots[0:1, :]
        for i in range(1, count):
            total = total + slots[i : i + 1, :]
        return total

    ring_step(1)
    for copy in bias:
        copy.wait()
    ezr[pl.ds(zl, 1), :] = ordered(esr, 4)
    mine = ezr.at[pl.ds(zl, 1)]
    enc = b_copy(mine, mine, 4, zpart)
    enc.start()
    bias = dec_stage(dx_r, ordered(dcore, 2), x, 5, xpeer)
    ring_step(2)
    for copy in bias:
        copy.wait()
    bias = dec_stage(dz_r, ordered(dx_r, 4), z, 8, zpeer)
    enc.wait()
    enc_out[...] = ezr[...]

    other = 1 - zl
    own_cols = zl * LAT

    def zcopy(k, way):
        cols = pl.ds(pl.multiple_of(way * 512, 512), 512)
        if k == 0:
            rows = pl.ds(pl.multiple_of(192 * other, 64), SUB)
        else:
            rows = pl.ds(pl.multiple_of(SUB * zl, 64), 192)
        return remote(
            zsend.at[rows, cols], zrecv.at[rows, cols],
            z_s.at[2 * k + way], z_r.at[2 * k + way], zpart,
        )

    for k in range(3):

        def finish(way, carry, k=k):
            i = 2 * k + way
            cols = pl.ds(pl.multiple_of(way * 512, 512), 512)
            out_cols = pl.ds(pl.multiple_of(own_cols + way * 512, 512), 512)
            part = partial(y, sub_of(k), way)
            ring(2, i).wait_recv()
            total = yrecv[2, i].astype(F32) + part
            if k == 0:
                rows = pl.ds(pl.multiple_of(192 * other, 64), SUB)
                zsend[rows, cols] = total.astype(BF16)
                zcopy(0, way).start()
            elif k == 1:
                tmp[...] = total
                theirs = tmp[pl.ds(pl.multiple_of(192 * other, 64), 192), :]
                zsend[pl.ds(pl.multiple_of(SUB * zl, 64), 192), cols] = theirs.astype(BF16)
                zcopy(1, way).start()
                ours = tmp[pl.ds(pl.multiple_of(192 * zl, 64), 192), :]
                wgrad[pl.ds(pl.multiple_of(SUB * other, 64), 192), out_cols] = ours
            else:
                wgrad[pl.ds(pl.multiple_of(192 * zl, 64), SUB), out_cols] = total
            return carry

        lax.fori_loop(0, 2, finish, 0)
        if k == 0:
            for copy in bias:
                copy.wait()
            bias = dec_stage(dy_r, ordered(dz_r, 4), y, 11, ypeer)
    for copy in bias:
        copy.wait()
    dec_out[...] = ordered(dy_r, 4)

    def drain(i, carry):
        for step in range(3):
            ring(step, i).wait_send()
        return carry

    lax.fori_loop(0, 6, drain, 0)
    for k in (0, 1):
        for way in (0, 1):
            zcopy(k, way).wait()

    def widen(j, carry):
        rows = pl.ds(pl.multiple_of(j * 96, 32), 96)
        wgrad[rows, pl.ds(pl.multiple_of(other * LAT, LAT), LAT)] = zrecv[rows, :].astype(F32)
        return carry

    lax.fori_loop(0, 6, widen, 0)


def per_device(attn_values, out_proj, post_gain, residual, sae_weight, enc_bias, dec_bias):
    vmem = pl.BlockSpec(memory_space=pltpu.VMEM)
    hbm = pl.BlockSpec(memory_space=pl.ANY)
    block = (4, 4, ROWS, D)
    dma = pltpu.SemaphoreType.DMA
    stream, wgrad, enc, dec = pl.pallas_call(
        kernel,
        out_shape=(
            jax.ShapeDtypeStruct((ROWS, D), BF16),
            jax.ShapeDtypeStruct((OWN, 2 * LAT), F32),
            jax.ShapeDtypeStruct((2, LAT), F32),
            jax.ShapeDtypeStruct((1, D), F32),
        ),
        in_specs=[vmem, vmem, vmem, vmem, hbm, vmem, vmem],
        out_specs=(vmem, vmem, vmem, vmem),
        scratch_shapes=[
            pltpu.VMEM((D, LAT), BF16),
            pltpu.VMEM((2,) + block, BF16),
            pltpu.VMEM((2,) + block, BF16),
            pltpu.VMEM((TOK, LAT), F32),
            pltpu.VMEM((TOK, LAT), BF16),
            pltpu.VMEM((TOK, LAT), BF16),
            pltpu.VMEM(block, BF16),
            pltpu.VMEM(block, F32),
            pltpu.VMEM(block, BF16),
            pltpu.VMEM((2, 4, ROWS, D), BF16),
            pltpu.VMEM((7, ROWS, D), BF16),
            pltpu.VMEM((3, 4, ROWS, HALF), BF16),
            pltpu.VMEM((3, 4, ROWS, HALF), BF16),
            pltpu.VMEM((4, ROWS, HALF), BF16),
            pltpu.VMEM((4, ROWS, HALF), BF16),
            pltpu.VMEM((3, ROWS, HALF), BF16),
            pltpu.VMEM((3, ROWS, HALF), BF16),
            pltpu.VMEM((6, SUB, 512), BF16),
            pltpu.VMEM((3, 6, SUB, 512), BF16),
            pltpu.VMEM((OWN, LAT), BF16),
            pltpu.VMEM((OWN, LAT), BF16),
            pltpu.VMEM((SUB, 512), F32),
            pltpu.VMEM((16, LAT), BF16),
            pltpu.VMEM((4, LAT), F32),
            pltpu.VMEM((2, LAT), F32),
            pltpu.VMEM((2, D), F32),
            pltpu.VMEM((4, D), F32),
            pltpu.VMEM((4, D), F32),
            pltpu.VMEM((4, D), F32),
            dma, dma, dma, dma((7,)), dma((7,)), dma((2, 21)), dma((2, 21)),
            dma((2,)), dma((2,)), dma((6,)), dma((6,)), dma((6,)), dma((6,)),
            dma((3, 6)), dma((3, 6)), dma((4,)), dma((4,)), dma((14,)), dma((14,)),
        ],
        compiler_params=pltpu.CompilerParams(
            collective_id=0, has_side_effects=True, vmem_limit_bytes=63 * 2**20
        ),
        cost_estimate=pl.CostEstimate(
            flops=25 * 10**9, bytes_accessed=20 * 10**6, transcendentals=0
        ),
    )(
        attn_values.reshape(2, 4, 2, ROWS, 256),
        out_proj,
        post_gain.reshape(1, D),
        residual,
        sae_weight,
        enc_bias.reshape(2, LAT),
        dec_bias.reshape(1, D),
    )
    return stream, wgrad, enc.reshape(2 * LAT), dec.reshape(D)


def solution(mesh):
    return jax.shard_map(
        per_device,
        mesh=mesh,
        in_specs=(
            P("dp", "mp"),
            P("mp", None),
            P(),
            P(("dp", "mp"), None),
            P(None, "mp"),
            P("mp"),
            P(),
        ),
        out_specs=(P(("dp", "mp"), None), P("dp", "mp"), P("mp"), P()),
        check_vma=False,
    )
```

```python
import math

import jax
import jax.numpy as jnp
from jax import lax
from jax.experimental import pallas as pl
from jax.experimental.pallas import tpu as pltpu
from jax.sharding import PartitionSpec as P

SPARSITY = 0.5
D = 4608
LAT = 1024
HALF = D // 2
ROWS = 16
TOK = 512
QROWS = D // 4
SUB = QROWS // 3
OWN = QROWS // 2
TOKENS = 2048
SCALE = 1.0 / math.sqrt(TOKENS)
F32 = jnp.float32
BF16 = jnp.bfloat16
H0 = pl.ds(0, HALF)
H1 = pl.ds(HALF, HALF)
LAST = (((1,), (1,)), ((), ()))
FIRST = (((0,), (0,)), ((), ()))


def kernel(
    attn, oproj, gain, resid, w_hbm, ebias, dbias,
    stream, own_grad, zrecv, enc_out, dec_out,
    w_v, cen, err, cen_y, err_y, pos, lat, pre, lat_y, pre_y,
    rsend, rown, rrecv, p1r2,
    rz, rx, s2a, s2b, r2a, r2b,
    zsend, tmp,
    es3, esr, ezr, dcore, dx_r, dz_r, dy_r,
    w_sem, p1_s, p1_r, p2_s, p2_r, ag_s, ag_r, rc_s, rc_r, r1_s, r1_r, r2_s, r2_r,
    yp_s, yp_r, yl_s, yl_r, y_s, y_r, z_s, z_r, b_s, b_r,
):
    dp, mp = lax.axis_index("dp"), lax.axis_index("mp")
    y, zl = dp // 2, dp % 2
    zh, x, c = mp // 8, (mp // 2) % 4, mp % 2
    z = zh * 2 + zl

    def dev(x_, y_, z_, c_):
        return (y_ * 2 + z_ % 2, (z_ // 2) * 8 + x_ * 2 + c_)

    core = dev(x, y, z, 1 - c)

    def xpeer(k):
        return dev((x + k) % 4, y, z, c)

    def zpeer(k):
        return dev(x, y, (z + k) % 4, c)

    def ypeer(k):
        return dev(x, (y + k) % 4, z, c)

    zpart = dev(x, y, zh * 2 + 1 - zl, c)

    def far(j):
        return dev((x + j % 4) % 4, y, ((zh + j // 4) % 2) * 2 + zl, c)

    def remote(src, dst, ssem, rsem, to):
        return pltpu.make_async_remote_copy(
            src_ref=src, dst_ref=dst, send_sem=ssem, recv_sem=rsem,
            device_id=to, device_id_type=pl.DeviceIdType.MESH,
        )

    w_copy = pltpu.make_async_copy(
        w_hbm.at[:, pl.ds(pl.multiple_of(zl * LAT, LAT), LAT)], w_v, w_sem
    )
    w_copy.start()

    barrier = pltpu.get_barrier_semaphore()
    partners = [core]
    for k in (1, 2, 3):
        partners += [xpeer(k), zpeer(k), ypeer(k), far(4 + k)]
    for to in partners:
        pl.semaphore_signal(barrier, inc=1, device_id=to, device_id_type=pl.DeviceIdType.MESH)
    pl.semaphore_wait(barrier, len(partners))

    def proj(which):
        return attn[:, :, pl.ds(which, 1)].reshape(128, 256)

    def peer_proj(j, carry):
        cols = pl.ds(pl.multiple_of(j * 512, 512), 512)
        part = jnp.dot(proj(1 - c), oproj[:, cols], preferred_element_type=F32)
        rsend[pl.ds(0, 2), :, :, cols] = part.astype(BF16).reshape(2, 4, ROWS, 512)
        return carry

    lax.fori_loop(0, 9, peer_proj, 0)
    p1 = remote(rsend.at[pl.ds(0, 2)], rrecv.at[pl.ds(0, 2)], p1_s, p1_r, core)
    p1.start()

    def own_proj(j, carry):
        cols = pl.ds(pl.multiple_of(j * 512, 512), 512)
        part = jnp.dot(proj(c), oproj[:, cols], preferred_element_type=F32)
        rown[pl.ds(0, 2), :, :, cols] = part.reshape(2, 4, ROWS, 512)
        return carry

    lax.fori_loop(0, 9, own_proj, 0)
    p1.wait()

    def add_proj(j, carry):
        total = rown[j // 4, j % 4] + rrecv[j // 4, j % 4].astype(F32)
        rown[j // 4, j % 4] = total
        rrecv[j // 4, j % 4] = total.astype(BF16)
        return carry

    lax.fori_loop(0, 8, add_proj, 0)
    p2 = [
        remote(
            rrecv.at[(zh + j // 4) % 2, (x + j % 4) % 4], p1r2.at[j - 1],
            p2_s.at[j - 1], p2_r.at[j - 1], far(j),
        )
        for j in range(1, 8)
    ]
    for copy in p2:
        copy.start()
    for copy in p2:
        copy.wait()
    attn_out = rown[zh, x]
    for j in range(7):
        attn_out = attn_out + p1r2[j].astype(F32)
    mean_sq = jnp.mean(attn_out * attn_out, axis=-1, keepdims=True)
    normed = attn_out * lax.rsqrt(mean_sq + 1e-06) * gain[...].reshape(1, D)
    shift = dbias[...].reshape(1, D)
    own_stream = (resid[...].astype(F32) + normed).astype(BF16)
    stream[...] = own_stream
    cen[c, z, x] = (own_stream.astype(F32) - shift).astype(BF16)

    def gather(at, cut, width, phase):
        left, right = pl.ds(0, cut), pl.ds(cut, width - cut)
        every = slice(None)

        def copy(ref, i, to):
            return remote(ref, ref, ag_s.at[phase, i], ag_r.at[phase, i], to)

        first, second, third = [], [], []

        def begin():
            for k in (1, 2, 3):
                first.append(copy(at(z, x, left), k, xpeer(k)))
                first.append(copy(at(z, x, right), 3 + k, zpeer(k)))
            for one in first:
                one.start()

        def spread():
            for one in first:
                one.wait()
            for k in (1, 2, 3):
                second.append(copy(at(z, every, left), 6 + k, zpeer(k)))
                second.append(copy(at(every, x, right), 9 + k, xpeer(k)))
            third.append(copy(at(z, every, left), 13, core))
            third.append(copy(at(every, x, right), 14, core))
            for one in second + third:
                one.start()

        def share():
            for k in (1, 2, 3):
                second[2 * k - 2].wait()
                third.append(copy(at((z + 4 - k) % 4, every, left), 14 + k, core))
                third[-1].start()
                second[2 * k - 1].wait()
                third.append(copy(at(every, (x + 4 - k) % 4, right), 17 + k, core))
                third[-1].start()

        def end():
            for one in third:
                one.wait()

        return begin, spread, share, end

    def columns_of(buf, buf_y, phase):
        out = []
        for k in (1, 2, 3):
            theirs = pl.ds(pl.multiple_of(((y + k) % 4) * QROWS, 128), QROWS)
            out.append(
                remote(
                    buf.at[c, z, x, :, theirs], buf_y.at[k - 1, c, z, x],
                    yp_s.at[phase, k - 1], yp_r.at[phase, k - 1], ypeer(k),
                )
            )
        for copy in out:
            copy.start()
        return out

    def gather_both(buf, buf_y, phase):
        whole = gather(lambda z_, x_, cols: buf.at[c, z_, x_, :, cols], HALF, D, phase)
        part = gather(
            lambda z_, x_, cols: buf_y.at[:, c, z_, x_, :, cols], 640, QROWS, 2 + phase
        )
        whole[0]()
        out = columns_of(buf, buf_y, phase)
        whole[1]()
        for copy in out:
            copy.wait()
        part[0]()
        whole[2]()
        whole[3]()
        part[1]()
        return part

    cen_part = gather_both(cen, cen_y, 0)
    w_copy.wait()

    bias_row = ebias[...].reshape(2, LAT)
    bias_row = jnp.where(zl == 0, bias_row[0:1], bias_row[1:2])
    ezr[0:1, :] = bias_row

    def encode(n, carry):
        cols = pl.ds(pl.multiple_of(n * 256, 256), 256)
        act = jnp.dot(cen[...].reshape(TOK, D), w_v[:, cols], preferred_element_type=F32)
        act = jnp.maximum(act + ezr[0:1, cols], 0.0)
        pos[:, cols] = act
        lat[:, cols] = (act * act).astype(BF16)
        return carry

    lax.fori_loop(0, 4, encode, 0)
    lat_out = [
        remote(lat, lat_y.at[k - 1], yl_s.at[k - 1], yl_r.at[k - 1], ypeer(k)) for k in (1, 2, 3)
    ]
    for copy in lat_out:
        copy.start()

    def decode(which, j):
        cols = pl.ds(pl.multiple_of(j * 256, 256), 256)
        rows = lat[pl.ds(pl.multiple_of(which * 256, 256), 256), :]
        part = lax.dot_general(rows, w_v[cols, :], LAST, preferred_element_type=F32)
        return cols, part.reshape(4, 4, ROWS, 256)

    def peer_decode(j, carry):
        cols, part = decode(1 - c, j)
        rsend[:, :, :, cols] = part.astype(BF16)
        return carry

    def own_decode(j, carry):
        cols, part = decode(c, j)
        rown[:, :, :, cols] = part
        return carry

    rc = []
    for h, cols in enumerate((H0, H1)):
        lax.fori_loop(9 * h, 9 * h + 9, peer_decode, 0)
        rc.append(
            remote(rsend.at[:, :, :, cols], rrecv.at[:, :, :, cols], rc_s.at[h], rc_r.at[h], core)
        )
        rc[-1].start()
    cen_part[2]()
    r1 = []
    for h, cols in enumerate((H0, H1)):
        lax.fori_loop(9 * h, 9 * h + 9, own_decode, 0)
        rc[h].wait()

        def add_decode(j, carry, cols=cols):
            total = rown[j // 4, j % 4, :, cols] + rrecv[j // 4, j % 4, :, cols].astype(F32)
            rown[j // 4, j % 4, :, cols] = total
            rrecv[j // 4, j % 4, :, cols] = total.astype(BF16)
            return carry

        lax.fori_loop(0, 16, add_decode, 0)
        for k in (1, 2, 3):
            if h == 0:
                src, dst, to = rrecv.at[(z + k) % 4, :, :, H0], rz.at[k - 1], zpeer(k)
            else:
                src, dst, to = rrecv.at[:, (x + k) % 4, :, H1], rx.at[k - 1], xpeer(k)
            i = 3 * h + k - 1
            r1.append(remote(src, dst, r1_s.at[i], r1_r.at[i], to))
            r1[-1].start()
    r2 = []
    for h in (0, 1):
        for k in (1, 2, 3):
            r1[3 * h + k - 1].wait()
        for i in range(4):
            if h == 0:
                total = rown[z, i, :, H0]
                for k in range(3):
                    total = total + rz[k, i].astype(F32)
                rown[z, i, :, H0] = total
                s2a[i] = total.astype(BF16)
            else:
                total = rown[i, x, :, H1]
                for k in range(3):
                    total = total + rx[k, i].astype(F32)
                rown[i, x, :, H1] = total
                s2b[i] = total.astype(BF16)
        for k in (1, 2, 3):
            if h == 0:
                src, dst, to = s2a.at[(x + k) % 4], r2a.at[k - 1], xpeer(k)
            else:
                src, dst, to = s2b.at[(z + k) % 4], r2b.at[k - 1], zpeer(k)
            i = 3 * h + k - 1
            r2.append(remote(src, dst, r2_s.at[i], r2_r.at[i], to))
            r2[-1].start()
    for h, cols in enumerate((H0, H1)):
        for k in (1, 2, 3):
            r2[3 * h + k - 1].wait()
        total = rown[z, x, :, cols]
        for k in range(3):
            total = total + (r2a, r2b)[h][k].astype(F32)
        grad = (total + shift[:, h * HALF : (h + 1) * HALF] - stream[:, cols].astype(F32)) * SCALE
        grad = grad.astype(BF16)
        err[c, z, x, :, cols] = grad
        dcore[pl.ds(c, 1), cols] = jnp.sum(grad.astype(F32), axis=0, keepdims=True)

    err_part = gather_both(err, err_y, 1)

    def back(n, carry):
        cols = pl.ds(pl.multiple_of(n * 256, 256), 256)
        grad = jnp.dot(err[...].reshape(TOK, D), w_v[:, cols], preferred_element_type=F32)
        grad = ((grad + SPARSITY * SCALE) * (2.0 * pos[:, cols])).astype(BF16)
        pre[:, cols] = grad
        esr[pl.ds(y, 1), cols] = jnp.sum(grad.astype(F32), axis=0, keepdims=True)
        return carry

    near, onward = [], []

    def ycopy(src, dst, n, i, to):
        return remote(src, dst, y_s.at[n, i], y_r.at[n, i], to)

    def send_near(n):
        cols = pl.ds(n * 256, 256)
        near.append(
            [
                ycopy(pre.at[:, cols], pre_y.at[0, :, cols], n, 0, ypeer(1)),
                ycopy(pre.at[:, cols], pre_y.at[2, :, cols], n, 1, ypeer(3)),
            ]
        )
        for copy in near[n]:
            copy.start()

    def send_onward(n):
        cols, top, low = pl.ds(n * 256, 256), pl.ds(0, 256), pl.ds(256, 256)
        onward.append(
            [
                ycopy(pre_y.at[0, top, cols], pre_y.at[1, top, cols], n, 2, ypeer(1)),
                ycopy(pre_y.at[2, low, cols], pre_y.at[1, low, cols], n, 3, ypeer(3)),
            ]
        )
        for copy, came in zip(onward[n], near[n]):
            came.wait()
            copy.start()

    lax.fori_loop(0, 1, back, 0)
    send_near(0)
    lax.fori_loop(1, 2, back, 0)
    send_near(1)
    lax.fori_loop(2, 4, back, 0)

    own_sum = esr[pl.ds(y, 1), :]
    high = own_sum.astype(BF16)
    rest = own_sum - high.astype(F32)
    mid = rest.astype(BF16)
    bottom = (rest - mid.astype(F32)).astype(BF16)
    es3[...] = jnp.concatenate([high, mid, bottom, jnp.zeros((13, LAT), BF16)], axis=0)

    def b_copy(src, dst, i, to):
        return remote(src, dst, b_s.at[i], b_r.at[i], to)

    bias = []
    mine = esr.at[pl.ds(y, 1)]
    for k in (1, 2, 3):
        bias.append(b_copy(mine, mine, k - 1, ypeer(k)))
    for copy in bias:
        copy.start()

    def project(j, carry):
        cols = pl.ds(pl.multiple_of(j * 512, 512), 512)
        part = lax.dot_general(es3[...], w_v[cols, :], LAST, preferred_element_type=F32)
        dcore[pl.ds(c, 1), cols] = dcore[pl.ds(c, 1), cols] - jnp.sum(part, axis=0, keepdims=True)
        return carry

    lax.fori_loop(0, 9, project, 0)
    mine = dcore.at[pl.ds(c, 1)]
    bias.append(b_copy(mine, mine, 3, core))
    bias[-1].start()

    def dec_stage(slots, value, me, first, peer):
        slots[pl.ds(me, 1), :] = value
        mine = slots.at[pl.ds(me, 1)]
        out = [b_copy(mine, mine, first + k, peer(k + 1)) for k in range(3)]
        for copy in out:
            copy.start()
        return out

    def ordered(slots, count):
        total = slots[0:1, :]
        for i in range(1, count):
            total = total + slots[i : i + 1, :]
        return total

    def grad_chunk(n):
        cols = pl.ds(n * 256, 256)

        def body(sub, carry):
            at = pl.ds(pl.multiple_of(sub * SUB, 128), SUB)
            own_at = pl.ds(pl.multiple_of(y * QROWS + sub * SUB, 128), SUB)

            def outer(rows, values):
                return lax.dot_general(
                    rows.reshape(TOK, SUB), values, FIRST, preferred_element_type=F32
                )

            total = outer(cen[:, :, :, :, own_at], pre[:, cols])
            total = total + outer(err[:, :, :, :, own_at], lat[:, cols])
            for k in range(3):
                total = total + outer(cen_y[k, :, :, :, :, at], pre_y[k, :, cols])
                total = total + outer(err_y[k, :, :, :, :, at], lat_y[k, :, cols])
            tmp[pl.ds(pl.multiple_of(sub * SUB, 128), SUB), :] = total
            return carry

        lax.fori_loop(0, 3, body, 0)
        theirs = pl.ds(pl.multiple_of((1 - zl) * OWN, 64), OWN)
        ours = pl.ds(pl.multiple_of(zl * OWN, 64), OWN)
        zsend[:, cols] = tmp[theirs, :].astype(BF16)
        copy = remote(zsend.at[:, cols], zrecv.at[:, cols], z_s.at[n], z_r.at[n], zpart)
        copy.start()
        own_grad[:, cols] = tmp[ours, :]
        return copy

    send_onward(0)
    send_near(2)
    err_part[2]()
    send_onward(1)
    send_near(3)
    cen_part[3]()
    err_part[3]()
    for copy in lat_out:
        copy.wait()
    for copy in bias:
        copy.wait()
    ezr[pl.ds(zl, 1), :] = ordered(esr, 4)
    mine = ezr.at[pl.ds(zl, 1)]
    enc = b_copy(mine, mine, 4, zpart)
    enc.start()
    bias = dec_stage(dx_r, ordered(dcore, 2), x, 5, xpeer)

    zout = []
    for n in range(4):
        if n in (1, 2):
            send_onward(n + 1)
        for copy in onward[n]:
            copy.wait()
        zout.append(grad_chunk(n))
        if n == 0:
            for copy in bias:
                copy.wait()
            bias = dec_stage(dz_r, ordered(dx_r, 4), z, 8, zpeer)
        elif n == 1:
            for copy in bias:
                copy.wait()
            bias = dec_stage(dy_r, ordered(dz_r, 4), y, 11, ypeer)
    enc.wait()
    enc_out[...] = ezr[...]
    for copy in bias:
        copy.wait()
    dec_out[...] = ordered(dy_r, 4)
    for copy in zout:
        copy.wait()


def write_out(stream, own_grad, their_grad, enc, dec, stream_out, wgrad, enc_out, dec_out):
    zl = lax.axis_index("dp") % 2
    here = pl.ds(pl.multiple_of(zl * LAT, LAT), LAT)
    there = pl.ds(pl.multiple_of((1 - zl) * LAT, LAT), LAT)
    wgrad[:, here] = own_grad[...]
    wgrad[:, there] = their_grad[...].astype(F32)

    @pl.when(pl.program_id(0) == 0)
    def _():
        stream_out[...] = stream[...]
        enc_out[pl.ds(0, LAT)] = enc[0, :]
        enc_out[pl.ds(LAT, LAT)] = enc[1, :]
        dec_out[...] = dec[0, :]


def per_device(attn_values, out_proj, post_gain, residual, sae_weight, enc_bias, dec_bias):
    vmem = pl.BlockSpec(memory_space=pltpu.VMEM)
    hbm = pl.BlockSpec(memory_space=pl.ANY)
    block = (4, 4, ROWS, D)
    dma = pltpu.SemaphoreType.DMA
    parts = pl.pallas_call(
        kernel,
        out_shape=(
            jax.ShapeDtypeStruct((ROWS, D), BF16),
            jax.ShapeDtypeStruct((OWN, LAT), F32),
            jax.ShapeDtypeStruct((OWN, LAT), BF16),
            jax.ShapeDtypeStruct((2, LAT), F32),
            jax.ShapeDtypeStruct((1, D), F32),
        ),
        in_specs=[vmem, vmem, vmem, vmem, hbm, vmem, vmem],
        out_specs=(vmem, vmem, vmem, vmem, vmem),
        scratch_shapes=[
            pltpu.VMEM((D, LAT), BF16),
            pltpu.VMEM((2,) + block, BF16),
            pltpu.VMEM((2,) + block, BF16),
            pltpu.VMEM((3, 2, 4, 4, ROWS, QROWS), BF16),
            pltpu.VMEM((3, 2, 4, 4, ROWS, QROWS), BF16),
            pltpu.VMEM((TOK, LAT), F32),
            pltpu.VMEM((TOK, LAT), BF16),
            pltpu.VMEM((TOK, LAT), BF16),
            pltpu.VMEM((3, TOK, LAT), BF16),
            pltpu.VMEM((3, TOK, LAT), BF16),
            pltpu.VMEM(block, BF16),
            pltpu.VMEM(block, F32),
            pltpu.VMEM(block, BF16),
            pltpu.VMEM((7, ROWS, D), BF16),
            pltpu.VMEM((3, 4, ROWS, HALF), BF16),
            pltpu.VMEM((3, 4, ROWS, HALF), BF16),
            pltpu.VMEM((4, ROWS, HALF), BF16),
            pltpu.VMEM((4, ROWS, HALF), BF16),
            pltpu.VMEM((3, ROWS, HALF), BF16),
            pltpu.VMEM((3, ROWS, HALF), BF16),
            pltpu.VMEM((OWN, LAT), BF16),
            pltpu.VMEM((QROWS, 256), F32),
            pltpu.VMEM((16, LAT), BF16),
            pltpu.VMEM((4, LAT), F32),
            pltpu.VMEM((2, LAT), F32),
            pltpu.VMEM((2, D), F32),
            pltpu.VMEM((4, D), F32),
            pltpu.VMEM((4, D), F32),
            pltpu.VMEM((4, D), F32),
            dma, dma, dma, dma((7,)), dma((7,)), dma((4, 21)), dma((4, 21)),
            dma((2,)), dma((2,)), dma((6,)), dma((6,)), dma((6,)), dma((6,)),
            dma((2, 3)), dma((2, 3)), dma((3,)), dma((3,)), dma((4, 4)), dma((4, 4)),
            dma((4,)), dma((4,)), dma((14,)), dma((14,)),
        ],
        compiler_params=pltpu.CompilerParams(
            collective_id=0, has_side_effects=True, vmem_limit_bytes=63 * 2**20
        ),
        cost_estimate=pl.CostEstimate(
            flops=25 * 10**9, bytes_accessed=20 * 10**6, transcendentals=0
        ),
    )(
        attn_values.reshape(2, 4, 2, ROWS, 256),
        out_proj, post_gain, residual, sae_weight, enc_bias, dec_bias,
    )
    steps = 6

    def fixed(*shape):
        return pl.BlockSpec(shape, lambda i: (0,) * len(shape))

    def rows(width):
        return pl.BlockSpec((OWN // steps, width), lambda i: (i, 0))

    return tuple(
        pl.pallas_call(
            write_out,
            grid=(steps,),
            out_shape=(
                jax.ShapeDtypeStruct((ROWS, D), BF16),
                jax.ShapeDtypeStruct((OWN, 2 * LAT), F32),
                jax.ShapeDtypeStruct((2 * LAT,), F32),
                jax.ShapeDtypeStruct((D,), F32),
            ),
            in_specs=[fixed(ROWS, D), rows(LAT), rows(LAT), fixed(2, LAT), fixed(1, D)],
            out_specs=(fixed(ROWS, D), rows(2 * LAT), fixed(2 * LAT), fixed(D)),
        )(*parts)
    )


def solution(mesh):
    return jax.shard_map(
        per_device,
        mesh=mesh,
        in_specs=(
            P("dp", "mp"),
            P("mp", None),
            P(),
            P(("dp", "mp"), None),
            P(None, "mp"),
            P("mp"),
            P(),
        ),
        out_specs=(P(("dp", "mp"), None), P("dp", "mp"), P("mp"), P()),
        check_vma=False,
    )
```

```python
import math

import jax
import jax.numpy as jnp
from jax import lax
from jax.experimental import pallas as pl
from jax.experimental.pallas import tpu as pltpu
from jax.sharding import PartitionSpec as P

SPARSITY = 0.5
D = 4608
LAT = 1024
HALF = D // 2
PART = HALF // 2
ROWS = 16
TOK = 512
BATCH = 256
QROWS = D // 4
SUB = QROWS // 3
OWN = QROWS // 2
TOKENS = 2048
SCALE = 1.0 / math.sqrt(TOKENS)
F32 = jnp.float32
BF16 = jnp.bfloat16
CUTS = (pl.ds(0, PART), pl.ds(PART, PART))
LAST = (((1,), (1,)), ((), ()))
FIRST = (((0,), (0,)), ((), ()))


def kernel(
    attn, oproj, gain, resid, w_hbm, ebias, dbias,
    stream, own_grad, zrecv, enc_out, dec_out,
    w_v, cen, err, cen_y, err_y, pos, lat, pre, lat_y, pre_y,
    rsend, rown, rrecv, p1r2,
    rz, rx, s2a, s2b, r2a, r2b,
    zsend, tmp, res2, str2, att, ssq, gain2, shift2,
    es3, esr, ezr, dcore, dx_r, dz_r, dy_r,
    w_sem, rs_s, rs_r, st_s, st_r, ss_s, ss_r, p1_s, p1_r, p2_s, p2_r, ag_s, ag_r,
    rc_s, rc_r, r1_s, r1_r, r2_s, r2_r,
    yp_s, yp_r, yl_s, yl_r, y_s, y_r, z_s, z_r, b_s, b_r,
):
    dp, mp = lax.axis_index("dp"), lax.axis_index("mp")
    y, zl = dp // 2, dp % 2
    zh, x, c = mp // 8, (mp // 2) % 4, mp % 2
    z = zh * 2 + zl

    def dev(x_, y_, z_, c_):
        return (y_ * 2 + z_ % 2, (z_ // 2) * 8 + x_ * 2 + c_)

    core = dev(x, y, z, 1 - c)

    def xpeer(k):
        return dev((x + k) % 4, y, z, c)

    def zpeer(k):
        return dev(x, y, (z + k) % 4, c)

    def ypeer(k):
        return dev(x, (y + k) % 4, z, c)

    zpart = dev(x, y, zh * 2 + 1 - zl, c)

    def far(j):
        return dev((x + j % 4) % 4, y, ((zh + j // 4) % 2) * 2 + zl, c)

    def remote(src, dst, ssem, rsem, to):
        return pltpu.make_async_remote_copy(
            src_ref=src, dst_ref=dst, send_sem=ssem, recv_sem=rsem,
            device_id=to, device_id_type=pl.DeviceIdType.MESH,
        )

    w_copy = pltpu.make_async_copy(
        w_hbm.at[:, pl.ds(pl.multiple_of(zl * LAT, LAT), LAT)], w_v, w_sem
    )
    w_copy.start()

    barrier = pltpu.get_barrier_semaphore()
    partners = [core]
    for k in (1, 2, 3):
        partners += [xpeer(k), zpeer(k), ypeer(k), far(4 + k)]
    for to in partners:
        pl.semaphore_signal(barrier, inc=1, device_id=to, device_id_type=pl.DeviceIdType.MESH)
    pl.semaphore_wait(barrier, len(partners))

    def half(which, at=0, width=HALF):
        return pl.ds(pl.multiple_of(which * HALF + at, 128), width)

    mine_cols, their_cols = half(c), half(1 - c)

    res_out = remote(resid.at[:, their_cols], res2.at[c], rs_s, rs_r, core)
    res_out.start()
    res2[c] = resid[:, mine_cols]
    row = gain[...].reshape(1, D)
    gain2[...] = jnp.where(c == 0, row[:, :HALF], row[:, HALF:])
    row = dbias[...].reshape(1, D)
    shift2[...] = jnp.where(c == 0, row[:, :HALF], row[:, HALF:])

    def proj(b, which, j):
        rows = attn[:, :, b].reshape(128, 256)
        part = jnp.dot(rows, oproj[:, half(which, j * 768, 768)], preferred_element_type=F32)
        return pl.ds(pl.multiple_of(j * 768, 768), 768), part.reshape(2, 4, ROWS, 768)

    p1, p2 = [], [[], []]
    for b in (0, 1):

        def peer_proj(j, carry, b=b):
            cols, part = proj(b, 1 - c, j)
            rsend[b, pl.ds(0, 2), :, :, cols] = part.astype(BF16)
            return carry

        lax.fori_loop(0, 3, peer_proj, 0)
        two = pl.ds(0, 2)
        p1.append(remote(rsend.at[b, two], rrecv.at[b, two], p1_s.at[b], p1_r.at[b], core))
        p1[b].start()
    for b in (0, 1):

        def own_proj(j, carry, b=b):
            cols, part = proj(b, c, j)
            rown[b, pl.ds(0, 2), :, :, cols] = part
            return carry

        lax.fori_loop(0, 3, own_proj, 0)
        p1[b].wait()

        def add_proj(j, carry, b=b):
            total = rown[b, j // 4, j % 4] + rrecv[b, j // 4, j % 4].astype(F32)
            rown[b, j // 4, j % 4] = total
            rrecv[b, j // 4, j % 4] = total.astype(BF16)
            return carry

        lax.fori_loop(0, 8, add_proj, 0)
        for j in range(1, 8):
            p2[b].append(
                remote(
                    rrecv.at[b, (zh + j // 4) % 2, (x + j % 4) % 4], p1r2.at[b, j - 1],
                    p2_s.at[b, j - 1], p2_r.at[b, j - 1], far(j),
                )
            )
            p2[b][-1].start()

    def gather(at, start, cut, width, phase):
        left = pl.ds(start, cut)
        right = pl.ds(start + cut, width - cut)
        if not isinstance(start, int):
            left = pl.ds(pl.multiple_of(start, 128), cut)
            right = pl.ds(pl.multiple_of(start + cut, 128), width - cut)
        every = slice(None)

        def copy(ref, i, to):
            return remote(ref, ref, ag_s.at[phase, i], ag_r.at[phase, i], to)

        first, second, third = [], [], []
        for k in (1, 2, 3):
            first.append(copy(at(z, x, left), k, xpeer(k)))
            first.append(copy(at(z, x, right), 3 + k, zpeer(k)))
            second.append(copy(at(z, every, left), 6 + k, zpeer(k)))
            second.append(copy(at(every, x, right), 9 + k, xpeer(k)))
        third.append(copy(at(z, every, left), 13, core))
        third.append(copy(at(every, x, right), 14, core))
        for k in (1, 2, 3):
            third.append(copy(at((z + 4 - k) % 4, every, left), 14 + k, core))
            third.append(copy(at(every, (x + 4 - k) % 4, right), 17 + k, core))

        def begin():
            for one in first:
                one.start()

        def spread():
            for one in first:
                one.wait()
            for one in second + third[:2]:
                one.start()

        def share():
            for came, one in zip(second, third[2:]):
                came.wait()
                one.start()

        def end():
            for one in third:
                one.wait()

        return begin, spread, share, end, third

    def rows_of(buf, b, phase):
        return gather(
            lambda z_, x_, cols: buf.at[b, z_, x_, :, cols], c * HALF, PART, HALF, phase
        )

    active = c == y // 2

    def part_of(buf, buf_y, b, phase):
        start, spread, share, end, third = gather(
            lambda z_, x_, cols: buf_y.at[:, b, z_, x_, :, cols], 0, 640, QROWS, 4 + phase
        )

        def piece(k, i):
            to = dev(x, (y + k) % 4, z, c)
            cols = pl.ds(pl.multiple_of(((y + k) % 4) * QROWS, 128), QROWS)
            return remote(
                buf.at[b, z, x, :, cols], buf_y.at[k - 1, b, z, x],
                yp_s.at[phase, i], yp_r.at[phase, k - 1], to,
            )

        def each(act):
            for i in (0, 1):
                k = (2 * c + i + 4 - y) % 4

                @pl.when(k > 0)
                def _(k=k, i=i):
                    act(piece(k, i))

        def send():
            each(lambda copy: copy.start())

        def begin():
            each(lambda copy: copy.wait_send())

            @pl.when(active)
            def _():
                for k in (1, 2, 3):
                    piece(k, 0).wait_recv()
                start()

        def when_active(step):
            def run():
                pl.when(active)(step)

            return run

        def finish():
            @pl.when(active)
            def _():
                for copy in third:
                    copy.wait_send()

            @pl.when(jnp.logical_not(active))
            def _():
                for copy in third:
                    copy.wait_recv()

        return send, begin, when_active(spread), when_active(share), finish

    squares = []

    def sum_squares(b):
        for copy in p2[b]:
            copy.wait()
        total = rown[b, zh, x]
        for j in range(7):
            total = total + p1r2[b, j].astype(F32)
        att[b] = total
        own_sq = jnp.sum(total * total, axis=-1, keepdims=True)
        ssq[b, c] = jnp.broadcast_to(own_sq, (ROWS, 128))
        mine = ssq.at[b, c]
        squares.append(remote(mine, mine, ss_s.at[b], ss_r.at[b], core))
        squares[b].start()

    def norm(b):
        squares[b].wait()
        mean_sq = (ssq[b, 0] + ssq[b, 1])[:, 0:1] * (1.0 / D)
        normed = att[b] * lax.rsqrt(mean_sq + 1e-06) * gain2[...]
        rows = (res2[b].astype(F32) + normed).astype(BF16)
        str2[b] = rows
        cen[b, z, x, :, mine_cols] = (rows.astype(F32) - shift2[...]).astype(BF16)

    cen_rows = [rows_of(cen, b, b) for b in (0, 1)]
    err_rows = [rows_of(err, b, 2 + b) for b in (0, 1)]
    cen_part = [part_of(cen, cen_y, b, b) for b in (0, 1)]
    err_part = [part_of(err, err_y, b, 2 + b) for b in (0, 1)]

    sum_squares(0)
    res_out.wait()
    norm(0)
    cen_rows[0][0]()
    cen_part[0][0]()
    sum_squares(1)
    norm(1)
    cen_rows[1][0]()
    cen_part[1][0]()
    stream_out = remote(str2.at[1 - c], stream.at[:, mine_cols], st_s, st_r, core)
    stream_out.start()
    stream[:, mine_cols] = str2[c]

    cen_rows[0][1]()
    cen_rows[1][1]()
    cen_part[0][1]()
    cen_part[1][1]()
    row = ebias[...].reshape(2, LAT)
    ezr[0:1, :] = jnp.where(zl == 0, row[0:1], row[1:2])
    w_copy.wait()

    def encode(b):
        def body(n, carry):
            cols = pl.ds(pl.multiple_of(n * 256, 256), 256)
            act = jnp.dot(
                cen[b].reshape(BATCH, D), w_v[:, cols], preferred_element_type=F32
            )
            act = jnp.maximum(act + ezr[0:1, cols], 0.0)
            pos[b, :, cols] = act
            lat[b, :, cols] = (act * act).astype(BF16)
            return carry

        lax.fori_loop(0, 4, body, 0)

    def round_y(own, got, cols, s_sem, r_sem):
        top, low = pl.ds(0, BATCH // 2), pl.ds(BATCH // 2, BATCH // 2)
        near = [
            remote(own.at[:, cols], got(0).at[:, cols], s_sem.at[0], r_sem.at[0], ypeer(1)),
            remote(own.at[:, cols], got(2).at[:, cols], s_sem.at[1], r_sem.at[1], ypeer(3)),
        ]
        on = [
            remote(
                got(0).at[top, cols], got(1).at[top, cols], s_sem.at[2], r_sem.at[2], ypeer(1)
            ),
            remote(
                got(2).at[low, cols], got(1).at[low, cols], s_sem.at[3], r_sem.at[3], ypeer(3)
            ),
        ]

        def begin():
            for copy in near:
                copy.start()

        def onward():
            for copy, came in zip(on, near):
                came.wait()
                copy.start()

        def end():
            for copy in on:
                copy.wait()

        return begin, onward, end

    lat_round = [
        round_y(
            lat.at[b], lambda k, b=b: lat_y.at[k, b], pl.ds(0, LAT), yl_s.at[b], yl_r.at[b]
        )
        for b in (0, 1)
    ]

    def decode(b, which, j):
        rows = half(which, j * 256, 256)
        part = lax.dot_general(lat[b], w_v[rows, :], LAST, preferred_element_type=F32)
        return pl.ds(pl.multiple_of(j * 256, 256), 256), part.reshape(4, 4, ROWS, 256)

    rc, r1, r2 = [], [[], []], [[], []]

    def decode_peer(b):
        def body(j, carry):
            cols, part = decode(b, 1 - c, j)
            rsend[b, :, :, :, cols] = part.astype(BF16)
            return carry

        lax.fori_loop(0, 9, body, 0)
        rc.append(remote(rsend.at[b], rrecv.at[b], rc_s.at[b], rc_r.at[b], core))
        rc[b].start()

    def decode_own(b):
        def body(j, carry):
            cols, part = decode(b, c, j)
            rown[b, :, :, :, cols] = part
            return carry

        lax.fori_loop(0, 9, body, 0)

    def recon_first(b):
        rc[b].wait()

        def body(j, carry):
            total = rown[b, j // 4, j % 4] + rrecv[b, j // 4, j % 4].astype(F32)
            rown[b, j // 4, j % 4] = total
            rrecv[b, j // 4, j % 4] = total.astype(BF16)
            return carry

        lax.fori_loop(0, 16, body, 0)
        for k in (1, 2, 3):
            for h in (0, 1):
                if h == 0:
                    src, dst, to = rrecv.at[b, (z + k) % 4, :, :, CUTS[0]], rz, zpeer(k)
                else:
                    src, dst, to = rrecv.at[b, :, (x + k) % 4, :, CUTS[1]], rx, xpeer(k)
                i = 2 * k - 2 + h
                r1[b].append(remote(src, dst.at[b, k - 1], r1_s.at[b, i], r1_r.at[b, i], to))
                r1[b][-1].start()

    def recon_second(b):
        for copy in r1[b]:
            copy.wait()
        for i in range(4):
            total = rown[b, z, i, :, CUTS[0]]
            for k in range(3):
                total = total + rz[b, k, i].astype(F32)
            rown[b, z, i, :, CUTS[0]] = total
            s2a[b, i] = total.astype(BF16)
            total = rown[b, i, x, :, CUTS[1]]
            for k in range(3):
                total = total + rx[b, k, i].astype(F32)
            rown[b, i, x, :, CUTS[1]] = total
            s2b[b, i] = total.astype(BF16)
        for k in (1, 2, 3):
            for h in (0, 1):
                if h == 0:
                    src, dst, to = s2a.at[b, (x + k) % 4], r2a, xpeer(k)
                else:
                    src, dst, to = s2b.at[b, (z + k) % 4], r2b, zpeer(k)
                i = 2 * k - 2 + h
                r2[b].append(remote(src, dst.at[b, k - 1], r2_s.at[b, i], r2_r.at[b, i], to))
                r2[b][-1].start()

    def error(b):
        for copy in r2[b]:
            copy.wait()
        for h in (0, 1):
            total = rown[b, z, x, :, CUTS[h]]
            for k in range(3):
                total = total + (r2a, r2b)[h][b, k].astype(F32)
            grad = total + shift2[:, CUTS[h]] - str2[b, :, CUTS[h]].astype(F32)
            grad = (grad * SCALE).astype(BF16)
            cols = half(c, h * PART, PART)
            err[b, z, x, :, cols] = grad
            sums = jnp.sum(grad.astype(F32), axis=0, keepdims=True)
            dcore[pl.ds(c, 1), cols] = dcore[pl.ds(c, 1), cols] + sums

    cen_rows[0][2]()
    cen_rows[0][3]()
    encode(0)
    lat_round[0][0]()
    cen_part[0][2]()
    decode_peer(0)
    decode_own(0)
    cen_rows[1][2]()
    recon_first(0)
    cen_rows[1][3]()
    encode(1)
    lat_round[1][0]()
    decode_peer(1)
    decode_own(1)
    recon_first(1)
    cen_part[1][2]()
    lat_round[0][1]()
    dcore[pl.ds(c, 1), :] = jnp.zeros((1, D), F32)
    recon_second(0)
    cen_part[0][3]()
    recon_second(1)
    error(0)
    err_rows[0][0]()
    err_part[0][0]()
    error(1)
    err_rows[1][0]()
    err_part[1][0]()
    cen_part[1][3]()
    err_rows[0][1]()
    err_rows[1][1]()
    lat_round[1][1]()
    err_part[0][1]()
    err_part[1][1]()
    err_rows[0][2]()
    err_rows[0][3]()

    def back(b):
        def body(n, carry):
            cols = pl.ds(pl.multiple_of(n * 256, 256), 256)
            grad = jnp.dot(
                err[b].reshape(BATCH, D), w_v[:, cols], preferred_element_type=F32
            )
            grad = ((grad + SPARSITY * SCALE) * (2.0 * pos[b, :, cols])).astype(BF16)
            pre[b, :, cols] = grad
            sums = jnp.sum(grad.astype(F32), axis=0, keepdims=True)
            if b == 1:
                sums = sums + esr[pl.ds(y, 1), cols]
            esr[pl.ds(y, 1), cols] = sums
            return carry

        lax.fori_loop(0, 4, body, 0)

    pre_round = [
        [
            round_y(
                pre.at[b], lambda k, b=b: pre_y.at[k, b], pl.ds(n * 256, 256),
                y_s.at[b, n], y_r.at[b, n],
            )
            for n in range(4)
        ]
        for b in (0, 1)
    ]
    back(0)
    for n in range(4):
        pre_round[0][n][0]()
    err_part[0][2]()
    err_rows[1][2]()
    err_rows[1][3]()
    back(1)
    pre_round[1][0][0]()
    pre_round[1][1][0]()
    err_part[1][2]()
    pre_round[0][0][1]()
    pre_round[0][1][1]()

    own_sum = esr[pl.ds(y, 1), :]
    high = own_sum.astype(BF16)
    rest = own_sum - high.astype(F32)
    mid = rest.astype(BF16)
    bottom = (rest - mid.astype(F32)).astype(BF16)
    es3[...] = jnp.concatenate([high, mid, bottom, jnp.zeros((13, LAT), BF16)], axis=0)

    def b_copy(src, dst, i, to):
        return remote(src, dst, b_s.at[i], b_r.at[i], to)

    bias = []
    mine = esr.at[pl.ds(y, 1)]
    for k in (1, 2, 3):
        bias.append(b_copy(mine, mine, k - 1, ypeer(k)))
    for copy in bias:
        copy.start()

    def project(j, carry):
        cols = pl.ds(pl.multiple_of(j * 512, 512), 512)
        part = lax.dot_general(es3[...], w_v[cols, :], LAST, preferred_element_type=F32)
        dcore[pl.ds(c, 1), cols] = dcore[pl.ds(c, 1), cols] - jnp.sum(part, axis=0, keepdims=True)
        return carry

    lax.fori_loop(0, 9, project, 0)
    mine = dcore.at[pl.ds(c, 1)]
    bias.append(b_copy(mine, mine, 3, core))
    bias[-1].start()

    def dec_stage(slots, value, me, first, peer):
        slots[pl.ds(me, 1), :] = value
        mine = slots.at[pl.ds(me, 1)]
        out = [b_copy(mine, mine, first + k, peer(k + 1)) for k in range(3)]
        for copy in out:
            copy.start()
        return out

    def ordered(slots, count):
        total = slots[0:1, :]
        for i in range(1, count):
            total = total + slots[i : i + 1, :]
        return total

    def grad_chunk(n):
        cols = pl.ds(n * 256, 256)

        def body(sub, carry):
            at = pl.ds(pl.multiple_of(sub * SUB, 128), SUB)
            own_at = pl.ds(pl.multiple_of(y * QROWS + sub * SUB, 128), SUB)

            def outer(rows, values):
                return lax.dot_general(
                    rows.reshape(TOK, SUB), values.reshape(TOK, 256), FIRST,
                    preferred_element_type=F32,
                )

            total = outer(cen[:, :, :, :, own_at], pre[:, :, cols])
            total = total + outer(err[:, :, :, :, own_at], lat[:, :, cols])
            for k in range(3):
                total = total + outer(cen_y[k, :, :, :, :, at], pre_y[k, :, :, cols])
                total = total + outer(err_y[k, :, :, :, :, at], lat_y[k, :, :, cols])
            tmp[pl.ds(pl.multiple_of(sub * SUB, 128), SUB), :] = total
            return carry

        lax.fori_loop(0, 3, body, 0)
        theirs = pl.ds(pl.multiple_of((1 - zl) * OWN, 64), OWN)
        ours = pl.ds(pl.multiple_of(zl * OWN, 64), OWN)
        zsend[:, cols] = tmp[theirs, :].astype(BF16)
        copy = remote(zsend.at[:, cols], zrecv.at[:, cols], z_s.at[n], z_r.at[n], zpart)
        copy.start()
        own_grad[:, cols] = tmp[ours, :]
        return copy

    pre_round[0][2][1]()
    pre_round[0][3][1]()
    for b in (0, 1):
        cen_part[b][4]()
    err_part[0][3]()
    pre_round[1][0][1]()
    pre_round[1][2][0]()
    err_part[1][3]()
    for copy in bias:
        copy.wait()
    ezr[pl.ds(zl, 1), :] = ordered(esr, 4)
    mine = ezr.at[pl.ds(zl, 1)]
    enc = b_copy(mine, mine, 4, zpart)
    enc.start()
    bias = dec_stage(dx_r, ordered(dcore, 2), x, 5, xpeer)
    pre_round[1][1][1]()
    pre_round[1][3][0]()
    for b in (0, 1):
        lat_round[b][2]()
        err_part[b][4]()

    zout = []
    for n in range(4):
        for b in (0, 1):
            pre_round[b][n][2]()
        zout.append(grad_chunk(n))
        if n < 2:
            pre_round[1][n + 2][1]()
        if n == 0:
            for copy in bias:
                copy.wait()
            bias = dec_stage(dz_r, ordered(dx_r, 4), z, 8, zpeer)
        elif n == 1:
            for copy in bias:
                copy.wait()
            bias = dec_stage(dy_r, ordered(dz_r, 4), y, 11, ypeer)
    stream_out.wait()
    enc.wait()
    enc_out[...] = ezr[...]
    for copy in bias:
        copy.wait()
    dec_out[...] = ordered(dy_r, 4)
    for copy in zout:
        copy.wait()


def write_out(stream, own_grad, their_grad, enc, dec, stream_out, wgrad, enc_out, dec_out):
    zl = lax.axis_index("dp") % 2
    here = pl.ds(pl.multiple_of(zl * LAT, LAT), LAT)
    there = pl.ds(pl.multiple_of((1 - zl) * LAT, LAT), LAT)
    wgrad[:, here] = own_grad[...]
    wgrad[:, there] = their_grad[...].astype(F32)

    @pl.when(pl.program_id(0) == 0)
    def _():
        stream_out[...] = stream[...]
        enc_out[pl.ds(0, LAT)] = enc[0, :]
        enc_out[pl.ds(LAT, LAT)] = enc[1, :]
        dec_out[...] = dec[0, :]


def per_device(attn_values, out_proj, post_gain, residual, sae_weight, enc_bias, dec_bias):
    vmem = pl.BlockSpec(memory_space=pltpu.VMEM)
    hbm = pl.BlockSpec(memory_space=pl.ANY)
    block = (2, 4, 4, ROWS, HALF)
    dma = pltpu.SemaphoreType.DMA
    parts = pl.pallas_call(
        kernel,
        out_shape=(
            jax.ShapeDtypeStruct((ROWS, D), BF16),
            jax.ShapeDtypeStruct((OWN, LAT), F32),
            jax.ShapeDtypeStruct((OWN, LAT), BF16),
            jax.ShapeDtypeStruct((2, LAT), F32),
            jax.ShapeDtypeStruct((1, D), F32),
        ),
        in_specs=[vmem, vmem, vmem, vmem, hbm, vmem, vmem],
        out_specs=(vmem, vmem, vmem, vmem, vmem),
        scratch_shapes=[
            pltpu.VMEM((D, LAT), BF16),
            pltpu.VMEM((2, 4, 4, ROWS, D), BF16),
            pltpu.VMEM((2, 4, 4, ROWS, D), BF16),
            pltpu.VMEM((3, 2, 4, 4, ROWS, QROWS), BF16),
            pltpu.VMEM((3, 2, 4, 4, ROWS, QROWS), BF16),
            pltpu.VMEM((2, BATCH, LAT), F32),
            pltpu.VMEM((2, BATCH, LAT), BF16),
            pltpu.VMEM((2, BATCH, LAT), BF16),
            pltpu.VMEM((3, 2, BATCH, LAT), BF16),
            pltpu.VMEM((3, 2, BATCH, LAT), BF16),
            pltpu.VMEM(block, BF16),
            pltpu.VMEM(block, F32),
            pltpu.VMEM(block, BF16),
            pltpu.VMEM((2, 7, ROWS, HALF), BF16),
            pltpu.VMEM((2, 3, 4, ROWS, PART), BF16),
            pltpu.VMEM((2, 3, 4, ROWS, PART), BF16),
            pltpu.VMEM((2, 4, ROWS, PART), BF16),
            pltpu.VMEM((2, 4, ROWS, PART), BF16),
            pltpu.VMEM((2, 3, ROWS, PART), BF16),
            pltpu.VMEM((2, 3, ROWS, PART), BF16),
            pltpu.VMEM((OWN, LAT), BF16),
            pltpu.VMEM((QROWS, 256), F32),
            pltpu.VMEM((2, ROWS, HALF), BF16),
            pltpu.VMEM((2, ROWS, HALF), BF16),
            pltpu.VMEM((2, ROWS, HALF), F32),
            pltpu.VMEM((2, 2, ROWS, 128), F32),
            pltpu.VMEM((1, HALF), F32),
            pltpu.VMEM((1, HALF), F32),
            pltpu.VMEM((16, LAT), BF16),
            pltpu.VMEM((4, LAT), F32),
            pltpu.VMEM((2, LAT), F32),
            pltpu.VMEM((2, D), F32),
            pltpu.VMEM((4, D), F32),
            pltpu.VMEM((4, D), F32),
            pltpu.VMEM((4, D), F32),
            dma, dma, dma, dma, dma, dma((2,)), dma((2,)), dma((2,)), dma((2,)),
            dma((2, 7)), dma((2, 7)), dma((8, 21)), dma((8, 21)),
            dma((2,)), dma((2,)), dma((2, 6)), dma((2, 6)), dma((2, 6)), dma((2, 6)),
            dma((4, 2)), dma((4, 3)), dma((2, 4)), dma((2, 4)), dma((2, 4, 4)), dma((2, 4, 4)),
            dma((4,)), dma((4,)), dma((14,)), dma((14,)),
        ],
        compiler_params=pltpu.CompilerParams(
            collective_id=0, has_side_effects=True, vmem_limit_bytes=63 * 2**20
        ),
        cost_estimate=pl.CostEstimate(
            flops=25 * 10**9, bytes_accessed=20 * 10**6, transcendentals=0
        ),
    )(
        attn_values.reshape(2, 4, 2, ROWS, 256),
        out_proj, post_gain, residual, sae_weight, enc_bias, dec_bias,
    )
    steps = 6

    def fixed(*shape):
        return pl.BlockSpec(shape, lambda i: (0,) * len(shape))

    def rows(width):
        return pl.BlockSpec((OWN // steps, width), lambda i: (i, 0))

    return tuple(
        pl.pallas_call(
            write_out,
            grid=(steps,),
            out_shape=(
                jax.ShapeDtypeStruct((ROWS, D), BF16),
                jax.ShapeDtypeStruct((OWN, 2 * LAT), F32),
                jax.ShapeDtypeStruct((2 * LAT,), F32),
                jax.ShapeDtypeStruct((D,), F32),
            ),
            in_specs=[fixed(ROWS, D), rows(LAT), rows(LAT), fixed(2, LAT), fixed(1, D)],
            out_specs=(fixed(ROWS, D), rows(2 * LAT), fixed(2 * LAT), fixed(D)),
        )(*parts)
    )


def solution(mesh):
    return jax.shard_map(
        per_device,
        mesh=mesh,
        in_specs=(
            P("dp", "mp"),
            P("mp", None),
            P(),
            P(("dp", "mp"), None),
            P(None, "mp"),
            P("mp"),
            P(),
        ),
        out_specs=(P(("dp", "mp"), None), P("dp", "mp"), P("mp"), P()),
        check_vma=False,
    )
```

```python
import math

import jax
import jax.numpy as jnp
from jax import lax
from jax.experimental import pallas as pl
from jax.experimental.pallas import tpu as pltpu
from jax.sharding import PartitionSpec as P

SPARSITY = 0.5
D = 4608
LAT = 1024
HALF = D // 2
PART = HALF // 2
ROWS = 16
TOK = 512
BATCH = 256
QROWS = D // 4
SUB = QROWS // 3
OWN = QROWS // 2
TOKENS = 2048
SCALE = 1.0 / math.sqrt(TOKENS)
F32 = jnp.float32
BF16 = jnp.bfloat16
CUTS = (pl.ds(0, PART), pl.ds(PART, PART))
LAST = (((1,), (1,)), ((), ()))
FIRST = (((0,), (0,)), ((), ()))


def kernel(
    attn, oproj, gain, resid, w_hbm, ebias, dbias,
    stream, own_grad, zrecv, enc_out, dec_out,
    w_v, cen, err, cen_y, err_y, pos, lat, pre, lat_y, pre_y,
    rsend, rown, rrecv, p1r2,
    rz, rx, s2a, s2b, r2a, r2b,
    zsend, tmp, res2, str2, att, ssq, gain2, shift2,
    es3, esr, ezr, dcore, dx_r, dz_r, dy_r,
    w_sem, rs_s, rs_r, st_s, st_r, ss_s, ss_r, p1_s, p1_r, p2_s, p2_r, ag_s, ag_r,
    rc_s, rc_r, r1_s, r1_r, r2_s, r2_r,
    yp_s, yp_r, yl_s, yl_r, y_s, y_r, z_s, z_r, b_s, b_r,
):
    dp, mp = lax.axis_index("dp"), lax.axis_index("mp")
    y, zl = dp // 2, dp % 2
    zh, x, c = mp // 8, (mp // 2) % 4, mp % 2
    z = zh * 2 + zl

    def dev(x_, y_, z_, c_):
        return (y_ * 2 + z_ % 2, (z_ // 2) * 8 + x_ * 2 + c_)

    core = dev(x, y, z, 1 - c)

    def xpeer(k):
        return dev((x + k) % 4, y, z, c)

    def zpeer(k):
        return dev(x, y, (z + k) % 4, c)

    def ypeer(k):
        return dev(x, (y + k) % 4, z, c)

    zpart = dev(x, y, zh * 2 + 1 - zl, c)

    def far(j):
        return dev((x + j % 4) % 4, y, ((zh + j // 4) % 2) * 2 + zl, c)

    def remote(src, dst, ssem, rsem, to):
        return pltpu.make_async_remote_copy(
            src_ref=src, dst_ref=dst, send_sem=ssem, recv_sem=rsem,
            device_id=to, device_id_type=pl.DeviceIdType.MESH,
        )

    w_copy = pltpu.make_async_copy(
        w_hbm.at[:, pl.ds(pl.multiple_of(zl * LAT, LAT), LAT)], w_v, w_sem
    )
    w_copy.start()

    barrier = pltpu.get_barrier_semaphore()
    partners = [core]
    for k in (1, 2, 3):
        partners += [xpeer(k), zpeer(k), ypeer(k), far(4 + k)]
    for to in partners:
        pl.semaphore_signal(barrier, inc=1, device_id=to, device_id_type=pl.DeviceIdType.MESH)
    pl.semaphore_wait(barrier, len(partners))

    def half(which, at=0, width=HALF):
        return pl.ds(pl.multiple_of(which * HALF + at, 128), width)

    mine_cols, their_cols = half(c), half(1 - c)

    res_out = remote(resid.at[:, their_cols], res2.at[c], rs_s, rs_r, core)
    res_out.start()
    res2[c] = resid[:, mine_cols]
    row = gain[...].reshape(1, D)
    gain2[...] = jnp.where(c == 0, row[:, :HALF], row[:, HALF:])
    row = dbias[...].reshape(1, D)
    shift2[...] = jnp.where(c == 0, row[:, :HALF], row[:, HALF:])

    def proj(b, which, j):
        rows = attn[:, :, b].reshape(128, 256)
        part = jnp.dot(rows, oproj[:, half(which, j * 768, 768)], preferred_element_type=F32)
        return pl.ds(pl.multiple_of(j * 768, 768), 768), part.reshape(2, 4, ROWS, 768)

    p1, p2 = [], [[], []]
    for b in (0, 1):

        def peer_proj(j, carry, b=b):
            cols, part = proj(b, 1 - c, j)
            rsend[b, pl.ds(0, 2), :, :, cols] = part.astype(BF16)
            return carry

        lax.fori_loop(0, 3, peer_proj, 0)
        two = pl.ds(0, 2)
        p1.append(remote(rsend.at[b, two], rrecv.at[b, two], p1_s.at[b], p1_r.at[b], core))
        p1[b].start()
    for b in (0, 1):

        def own_proj(j, carry, b=b):
            cols, part = proj(b, c, j)
            rown[b, pl.ds(0, 2), :, :, cols] = part
            return carry

        lax.fori_loop(0, 3, own_proj, 0)
        p1[b].wait()

        def add_proj(j, carry, b=b):
            total = rown[b, j // 4, j % 4] + rrecv[b, j // 4, j % 4].astype(F32)
            rown[b, j // 4, j % 4] = total
            rrecv[b, j // 4, j % 4] = total.astype(BF16)
            return carry

        lax.fori_loop(0, 8, add_proj, 0)
        for j in range(1, 8):
            p2[b].append(
                remote(
                    rrecv.at[b, (zh + j // 4) % 2, (x + j % 4) % 4], p1r2.at[b, j - 1],
                    p2_s.at[b, j - 1], p2_r.at[b, j - 1], far(j),
                )
            )
            p2[b][-1].start()

    def gather(at, start, cut, width, phase):
        left = pl.ds(start, cut)
        right = pl.ds(start + cut, width - cut)
        if not isinstance(start, int):
            left = pl.ds(pl.multiple_of(start, 128), cut)
            right = pl.ds(pl.multiple_of(start + cut, 128), width - cut)
        every = slice(None)

        def copy(ref, i, to):
            return remote(ref, ref, ag_s.at[phase, i], ag_r.at[phase, i], to)

        first, second, third = [], [], []
        for k in (1, 2, 3):
            first.append(copy(at(z, x, left), k, xpeer(k)))
            first.append(copy(at(z, x, right), 3 + k, zpeer(k)))
            second.append(copy(at(z, every, left), 6 + k, zpeer(k)))
            second.append(copy(at(every, x, right), 9 + k, xpeer(k)))
        third.append(copy(at(z, every, left), 13, core))
        third.append(copy(at(every, x, right), 14, core))
        for k in (1, 2, 3):
            third.append(copy(at((z + 4 - k) % 4, every, left), 14 + k, core))
            third.append(copy(at(every, (x + 4 - k) % 4, right), 17 + k, core))

        def begin():
            for one in first:
                one.start()

        def spread():
            for one in first:
                one.wait()
            for one in second + third[:2]:
                one.start()

        def share():
            for came, one in zip(second, third[2:]):
                came.wait()
                one.start()

        def end():
            for one in third:
                one.wait()

        return begin, spread, share, end, third

    def rows_of(buf, b, phase):
        return gather(
            lambda z_, x_, cols: buf.at[b, z_, x_, :, cols], c * HALF, PART, HALF, phase
        )

    active = c == y // 2

    def part_of(buf, buf_y, b, phase):
        start, spread, share, end, third = gather(
            lambda z_, x_, cols: buf_y.at[:, b, z_, x_, :, cols], 0, 640, QROWS, 4 + phase
        )

        def piece(k, i):
            to = dev(x, (y + k) % 4, z, c)
            cols = pl.ds(pl.multiple_of(((y + k) % 4) * QROWS, 128), QROWS)
            return remote(
                buf.at[b, z, x, :, cols], buf_y.at[k - 1, b, z, x],
                yp_s.at[phase, i], yp_r.at[phase, k - 1], to,
            )

        def each(act):
            for i in (0, 1):
                k = (2 * c + i + 4 - y) % 4

                @pl.when(k > 0)
                def _(k=k, i=i):
                    act(piece(k, i))

        def send():
            each(lambda copy: copy.start())

        def begin():
            each(lambda copy: copy.wait_send())

            @pl.when(active)
            def _():
                for k in (1, 2, 3):
                    piece(k, 0).wait_recv()
                start()

        def when_active(step):
            def run():
                pl.when(active)(step)

            return run

        def finish():
            @pl.when(active)
            def _():
                for copy in third:
                    copy.wait_send()

            @pl.when(jnp.logical_not(active))
            def _():
                for copy in third:
                    copy.wait_recv()

        return send, begin, when_active(spread), when_active(share), finish

    squares = []

    def sum_squares(b):
        for copy in p2[b]:
            copy.wait()
        total = rown[b, zh, x]
        for j in range(7):
            total = total + p1r2[b, j].astype(F32)
        att[b] = total
        own_sq = jnp.sum(total * total, axis=-1, keepdims=True)
        ssq[b, c] = jnp.broadcast_to(own_sq, (ROWS, 128))
        mine = ssq.at[b, c]
        squares.append(remote(mine, mine, ss_s.at[b], ss_r.at[b], core))
        squares[b].start()

    def norm(b):
        squares[b].wait()
        mean_sq = (ssq[b, 0] + ssq[b, 1])[:, 0:1] * (1.0 / D)
        normed = att[b] * lax.rsqrt(mean_sq + 1e-06) * gain2[...]
        rows = (res2[b].astype(F32) + normed).astype(BF16)
        str2[b] = rows
        cen[b, z, x, :, mine_cols] = (rows.astype(F32) - shift2[...]).astype(BF16)

    cen_rows = [rows_of(cen, b, b) for b in (0, 1)]
    err_rows = [rows_of(err, b, 2 + b) for b in (0, 1)]
    cen_part = [part_of(cen, cen_y, b, b) for b in (0, 1)]
    err_part = [part_of(err, err_y, b, 2 + b) for b in (0, 1)]

    sum_squares(0)
    res_out.wait()
    norm(0)
    cen_rows[0][0]()
    cen_part[0][0]()
    sum_squares(1)
    norm(1)
    cen_rows[1][0]()
    cen_part[1][0]()
    stream_out = remote(str2.at[1 - c], stream.at[:, mine_cols], st_s, st_r, core)
    stream_out.start()
    stream[:, mine_cols] = str2[c]

    cen_rows[0][1]()
    cen_rows[1][1]()
    cen_part[0][1]()
    cen_part[1][1]()
    row = ebias[...].reshape(2, LAT)
    ezr[0:1, :] = jnp.where(zl == 0, row[0:1], row[1:2])
    w_copy.wait()

    def encode(b):
        def body(n, carry):
            cols = pl.ds(pl.multiple_of(n * 256, 256), 256)
            act = jnp.dot(
                cen[b].reshape(BATCH, D), w_v[:, cols], preferred_element_type=F32
            )
            act = jnp.maximum(act + ezr[0:1, cols], 0.0)
            pos[b, :, cols] = act
            lat[b, :, cols] = (act * act).astype(BF16)
            return carry

        lax.fori_loop(0, 4, body, 0)

    def round_y(own, got, cols, s_sem, r_sem):
        top, low = pl.ds(0, BATCH // 2), pl.ds(BATCH // 2, BATCH // 2)
        near = [
            remote(own.at[:, cols], got(0).at[:, cols], s_sem.at[0], r_sem.at[0], ypeer(1)),
            remote(own.at[:, cols], got(2).at[:, cols], s_sem.at[1], r_sem.at[1], ypeer(3)),
        ]
        on = [
            remote(
                got(0).at[top, cols], got(1).at[top, cols], s_sem.at[2], r_sem.at[2], ypeer(1)
            ),
            remote(
                got(2).at[low, cols], got(1).at[low, cols], s_sem.at[3], r_sem.at[3], ypeer(3)
            ),
        ]

        def begin():
            for copy in near:
                copy.start()

        def onward():
            for copy, came in zip(on, near):
                came.wait()
                copy.start()

        def end():
            for copy in on:
                copy.wait()

        return begin, onward, end

    lat_round = [
        round_y(
            lat.at[b], lambda k, b=b: lat_y.at[k, b], pl.ds(0, LAT), yl_s.at[b], yl_r.at[b]
        )
        for b in (0, 1)
    ]

    def decode(b, which, j):
        rows = half(which, j * 256, 256)
        part = lax.dot_general(lat[b], w_v[rows, :], LAST, preferred_element_type=F32)
        return pl.ds(pl.multiple_of(j * 256, 256), 256), part.reshape(4, 4, ROWS, 256)

    rc, r1, r2 = [], [[], []], [[], []]

    def decode_peer(b):
        def body(j, carry):
            cols, part = decode(b, 1 - c, j)
            rsend[b, :, :, :, cols] = part.astype(BF16)
            return carry

        lax.fori_loop(0, 9, body, 0)
        rc.append(remote(rsend.at[b], rrecv.at[b], rc_s.at[b], rc_r.at[b], core))
        rc[b].start()

    def decode_own(b):
        def body(j, carry):
            cols, part = decode(b, c, j)
            rown[b, :, :, :, cols] = part
            return carry

        lax.fori_loop(0, 9, body, 0)

    def recon_first(b):
        rc[b].wait()

        def body(j, carry):
            total = rown[b, j // 4, j % 4] + rrecv[b, j // 4, j % 4].astype(F32)
            rown[b, j // 4, j % 4] = total
            rrecv[b, j // 4, j % 4] = total.astype(BF16)
            return carry

        lax.fori_loop(0, 16, body, 0)
        for k in (1, 2, 3):
            for h in (0, 1):
                if h == 0:
                    src, dst, to = rrecv.at[b, (z + k) % 4, :, :, CUTS[0]], rz, zpeer(k)
                else:
                    src, dst, to = rrecv.at[b, :, (x + k) % 4, :, CUTS[1]], rx, xpeer(k)
                i = 2 * k - 2 + h
                r1[b].append(remote(src, dst.at[b, k - 1], r1_s.at[b, i], r1_r.at[b, i], to))
                r1[b][-1].start()

    def recon_second(b):
        for copy in r1[b]:
            copy.wait()
        for i in range(4):
            total = rown[b, z, i, :, CUTS[0]]
            for k in range(3):
                total = total + rz[b, k, i].astype(F32)
            rown[b, z, i, :, CUTS[0]] = total
            s2a[b, i] = total.astype(BF16)
            total = rown[b, i, x, :, CUTS[1]]
            for k in range(3):
                total = total + rx[b, k, i].astype(F32)
            rown[b, i, x, :, CUTS[1]] = total
            s2b[b, i] = total.astype(BF16)
        for k in (1, 2, 3):
            for h in (0, 1):
                if h == 0:
                    src, dst, to = s2a.at[b, (x + k) % 4], r2a, xpeer(k)
                else:
                    src, dst, to = s2b.at[b, (z + k) % 4], r2b, zpeer(k)
                i = 2 * k - 2 + h
                r2[b].append(remote(src, dst.at[b, k - 1], r2_s.at[b, i], r2_r.at[b, i], to))
                r2[b][-1].start()

    def error(b):
        for copy in r2[b]:
            copy.wait()
        for h in (0, 1):
            total = rown[b, z, x, :, CUTS[h]]
            for k in range(3):
                total = total + (r2a, r2b)[h][b, k].astype(F32)
            grad = total + shift2[:, CUTS[h]] - str2[b, :, CUTS[h]].astype(F32)
            grad = (grad * SCALE).astype(BF16)
            cols = half(c, h * PART, PART)
            err[b, z, x, :, cols] = grad
            sums = jnp.sum(grad.astype(F32), axis=0, keepdims=True)
            dcore[pl.ds(c, 1), cols] = dcore[pl.ds(c, 1), cols] + sums

    cen_rows[0][2]()
    cen_rows[0][3]()
    encode(0)
    lat_round[0][0]()
    cen_part[0][2]()
    decode_peer(0)
    decode_own(0)
    cen_rows[1][2]()
    recon_first(0)
    cen_rows[1][3]()
    encode(1)
    lat_round[1][0]()
    decode_peer(1)
    decode_own(1)
    recon_first(1)
    cen_part[1][2]()
    lat_round[0][1]()
    dcore[pl.ds(c, 1), :] = jnp.zeros((1, D), F32)
    recon_second(0)
    cen_part[0][3]()
    recon_second(1)
    error(0)
    err_rows[0][0]()
    err_part[0][0]()
    error(1)
    err_rows[1][0]()
    err_part[1][0]()
    cen_part[1][3]()
    err_rows[0][1]()
    err_rows[1][1]()
    lat_round[1][1]()
    err_part[0][1]()
    err_part[1][1]()
    err_rows[0][2]()
    err_rows[0][3]()

    def back(b):
        def body(n, carry):
            cols = pl.ds(pl.multiple_of(n * 256, 256), 256)
            grad = jnp.dot(
                err[b].reshape(BATCH, D), w_v[:, cols], preferred_element_type=F32
            )
            grad = ((grad + SPARSITY * SCALE) * (2.0 * pos[b, :, cols])).astype(BF16)
            pre[b, n] = grad
            sums = jnp.sum(grad.astype(F32), axis=0, keepdims=True)
            if b == 1:
                sums = sums + esr[pl.ds(y, 1), cols]
            esr[pl.ds(y, 1), cols] = sums
            return carry

        lax.fori_loop(0, 4, body, 0)

    pre_round = [
        [
            round_y(
                pre.at[b, n], lambda k, b=b, n=n: pre_y.at[k, b, n], pl.ds(0, 256),
                y_s.at[b, n], y_r.at[b, n],
            )
            for n in range(4)
        ]
        for b in (0, 1)
    ]
    back(0)
    pre_round[0][0][0]()
    pre_round[0][1][0]()
    err_part[0][2]()
    err_rows[1][2]()
    err_rows[1][3]()
    back(1)
    pre_round[1][0][0]()
    pre_round[1][1][0]()
    err_part[1][2]()
    pre_round[0][0][1]()
    pre_round[0][1][1]()

    own_sum = esr[pl.ds(y, 1), :]
    high = own_sum.astype(BF16)
    rest = own_sum - high.astype(F32)
    mid = rest.astype(BF16)
    bottom = (rest - mid.astype(F32)).astype(BF16)
    es3[...] = jnp.concatenate([high, mid, bottom, jnp.zeros((13, LAT), BF16)], axis=0)

    def b_copy(src, dst, i, to):
        return remote(src, dst, b_s.at[i], b_r.at[i], to)

    bias = []
    mine = esr.at[pl.ds(y, 1)]
    for k in (1, 2, 3):
        bias.append(b_copy(mine, mine, k - 1, ypeer(k)))
    for copy in bias:
        copy.start()

    def project(j, carry):
        cols = pl.ds(pl.multiple_of(j * 512, 512), 512)
        part = lax.dot_general(es3[...], w_v[cols, :], LAST, preferred_element_type=F32)
        dcore[pl.ds(c, 1), cols] = dcore[pl.ds(c, 1), cols] - jnp.sum(part, axis=0, keepdims=True)
        return carry

    def dec_stage(slots, value, me, first, peer):
        slots[pl.ds(me, 1), :] = value
        mine = slots.at[pl.ds(me, 1)]
        out = [b_copy(mine, mine, first + k, peer(k + 1)) for k in range(3)]
        for copy in out:
            copy.start()
        return out

    def ordered(slots, count):
        total = slots[0:1, :]
        for i in range(1, count):
            total = total + slots[i : i + 1, :]
        return total

    def grad_chunk(n):
        cols = pl.ds(n * 256, 256)

        def body(sub, carry):
            at = pl.ds(pl.multiple_of(sub * SUB, 128), SUB)
            own_at = pl.ds(pl.multiple_of(y * QROWS + sub * SUB, 128), SUB)

            def outer(rows, values):
                return lax.dot_general(
                    rows.reshape(TOK, SUB), values.reshape(TOK, 256), FIRST,
                    preferred_element_type=F32,
                )

            total = outer(cen[:, :, :, :, own_at], pre[:, n])
            total = total + outer(err[:, :, :, :, own_at], lat[:, :, cols])
            for k in range(3):
                total = total + outer(cen_y[k, :, :, :, :, at], pre_y[k, :, n])
                total = total + outer(err_y[k, :, :, :, :, at], lat_y[k, :, :, cols])
            tmp[pl.ds(pl.multiple_of(sub * SUB, 128), SUB), :] = total
            return carry

        lax.fori_loop(0, 3, body, 0)
        theirs = pl.ds(pl.multiple_of((1 - zl) * OWN, 64), OWN)
        ours = pl.ds(pl.multiple_of(zl * OWN, 64), OWN)
        zsend[n] = tmp[theirs, :].astype(BF16)
        copy = remote(zsend.at[n], zrecv.at[n], z_s.at[n], z_r.at[n], zpart)
        copy.start()
        own_grad[:, cols] = tmp[ours, :]
        return copy

    pre_round[1][0][1]()
    pre_round[0][2][0]()
    pre_round[1][2][0]()
    err_part[0][3]()
    pre_round[1][1][1]()
    pre_round[0][3][0]()
    pre_round[1][3][0]()
    err_part[1][3]()
    for b in (0, 1):
        cen_part[b][4]()
        lat_round[b][2]()
        err_part[b][4]()

    zout = []
    for n in range(4):
        for b in (0, 1):
            pre_round[b][n][2]()
        zout.append(grad_chunk(n))
        if n < 2:
            for b in (0, 1):
                pre_round[b][n + 2][1]()
        for copy in bias:
            copy.wait()
        if n == 0:
            ezr[pl.ds(zl, 1), :] = ordered(esr, 4)
            mine = ezr.at[pl.ds(zl, 1)]
            enc = b_copy(mine, mine, 4, zpart)
            enc.start()
            lax.fori_loop(0, 9, project, 0)
            mine = dcore.at[pl.ds(c, 1)]
            bias = [b_copy(mine, mine, 3, core)]
            bias[0].start()
        elif n == 1:
            bias = dec_stage(dx_r, ordered(dcore, 2), x, 5, xpeer)
        elif n == 2:
            bias = dec_stage(dz_r, ordered(dx_r, 4), z, 8, zpeer)
        else:
            bias = dec_stage(dy_r, ordered(dz_r, 4), y, 11, ypeer)
    stream_out.wait()
    enc.wait()
    enc_out[...] = ezr[...]
    for copy in bias:
        copy.wait()
    dec_out[...] = ordered(dy_r, 4)
    for copy in zout:
        copy.wait()


def write_out(stream, own_grad, their_grad, enc, dec, stream_out, wgrad, enc_out, dec_out):
    zl = lax.axis_index("dp") % 2
    here = pl.ds(pl.multiple_of(zl * LAT, LAT), LAT)
    wgrad[:, here] = own_grad[...]
    for n in range(4):
        there = pl.ds(pl.multiple_of((1 - zl) * LAT + n * 256, 256), 256)
        wgrad[:, there] = their_grad[n].astype(F32)

    @pl.when(pl.program_id(0) == 0)
    def _():
        stream_out[...] = stream[...]
        enc_out[pl.ds(0, LAT)] = enc[0, :]
        enc_out[pl.ds(LAT, LAT)] = enc[1, :]
        dec_out[...] = dec[0, :]


def per_device(attn_values, out_proj, post_gain, residual, sae_weight, enc_bias, dec_bias):
    vmem = pl.BlockSpec(memory_space=pltpu.VMEM)
    hbm = pl.BlockSpec(memory_space=pl.ANY)
    block = (2, 4, 4, ROWS, HALF)
    dma = pltpu.SemaphoreType.DMA
    parts = pl.pallas_call(
        kernel,
        out_shape=(
            jax.ShapeDtypeStruct((ROWS, D), BF16),
            jax.ShapeDtypeStruct((OWN, LAT), F32),
            jax.ShapeDtypeStruct((4, OWN, 256), BF16),
            jax.ShapeDtypeStruct((2, LAT), F32),
            jax.ShapeDtypeStruct((1, D), F32),
        ),
        in_specs=[vmem, vmem, vmem, vmem, hbm, vmem, vmem],
        out_specs=(vmem, vmem, vmem, vmem, vmem),
        scratch_shapes=[
            pltpu.VMEM((D, LAT), BF16),
            pltpu.VMEM((2, 4, 4, ROWS, D), BF16),
            pltpu.VMEM((2, 4, 4, ROWS, D), BF16),
            pltpu.VMEM((3, 2, 4, 4, ROWS, QROWS), BF16),
            pltpu.VMEM((3, 2, 4, 4, ROWS, QROWS), BF16),
            pltpu.VMEM((2, BATCH, LAT), F32),
            pltpu.VMEM((2, BATCH, LAT), BF16),
            pltpu.VMEM((2, 4, BATCH, 256), BF16),
            pltpu.VMEM((3, 2, BATCH, LAT), BF16),
            pltpu.VMEM((3, 2, 4, BATCH, 256), BF16),
            pltpu.VMEM(block, BF16),
            pltpu.VMEM(block, F32),
            pltpu.VMEM(block, BF16),
            pltpu.VMEM((2, 7, ROWS, HALF), BF16),
            pltpu.VMEM((2, 3, 4, ROWS, PART), BF16),
            pltpu.VMEM((2, 3, 4, ROWS, PART), BF16),
            pltpu.VMEM((2, 4, ROWS, PART), BF16),
            pltpu.VMEM((2, 4, ROWS, PART), BF16),
            pltpu.VMEM((2, 3, ROWS, PART), BF16),
            pltpu.VMEM((2, 3, ROWS, PART), BF16),
            pltpu.VMEM((4, OWN, 256), BF16),
            pltpu.VMEM((QROWS, 256), F32),
            pltpu.VMEM((2, ROWS, HALF), BF16),
            pltpu.VMEM((2, ROWS, HALF), BF16),
            pltpu.VMEM((2, ROWS, HALF), F32),
            pltpu.VMEM((2, 2, ROWS, 128), F32),
            pltpu.VMEM((1, HALF), F32),
            pltpu.VMEM((1, HALF), F32),
            pltpu.VMEM((16, LAT), BF16),
            pltpu.VMEM((4, LAT), F32),
            pltpu.VMEM((2, LAT), F32),
            pltpu.VMEM((2, D), F32),
            pltpu.VMEM((4, D), F32),
            pltpu.VMEM((4, D), F32),
            pltpu.VMEM((4, D), F32),
            dma, dma, dma, dma, dma, dma((2,)), dma((2,)), dma((2,)), dma((2,)),
            dma((2, 7)), dma((2, 7)), dma((8, 21)), dma((8, 21)),
            dma((2,)), dma((2,)), dma((2, 6)), dma((2, 6)), dma((2, 6)), dma((2, 6)),
            dma((4, 2)), dma((4, 3)), dma((2, 4)), dma((2, 4)), dma((2, 4, 4)), dma((2, 4, 4)),
            dma((4,)), dma((4,)), dma((14,)), dma((14,)),
        ],
        compiler_params=pltpu.CompilerParams(
            collective_id=0, has_side_effects=True, vmem_limit_bytes=63 * 2**20
        ),
        cost_estimate=pl.CostEstimate(
            flops=25 * 10**9, bytes_accessed=20 * 10**6, transcendentals=0
        ),
    )(
        attn_values.reshape(2, 4, 2, ROWS, 256),
        out_proj, post_gain, residual, sae_weight, enc_bias, dec_bias,
    )
    steps = 3

    def fixed(*shape):
        return pl.BlockSpec(shape, lambda i: (0,) * len(shape))

    def rows(width):
        return pl.BlockSpec((OWN // steps, width), lambda i: (i, 0))

    return tuple(
        pl.pallas_call(
            write_out,
            grid=(steps,),
            out_shape=(
                jax.ShapeDtypeStruct((ROWS, D), BF16),
                jax.ShapeDtypeStruct((OWN, 2 * LAT), F32),
                jax.ShapeDtypeStruct((2 * LAT,), F32),
                jax.ShapeDtypeStruct((D,), F32),
            ),
            in_specs=[
                fixed(ROWS, D),
                rows(LAT),
                pl.BlockSpec((4, OWN // steps, 256), lambda i: (0, i, 0)),
                fixed(2, LAT),
                fixed(1, D),
            ],
            out_specs=(fixed(ROWS, D), rows(2 * LAT), fixed(2 * LAT), fixed(D)),
        )(*parts)
    )


def solution(mesh):
    return jax.shard_map(
        per_device,
        mesh=mesh,
        in_specs=(
            P("dp", "mp"),
            P("mp", None),
            P(),
            P(("dp", "mp"), None),
            P(None, "mp"),
            P("mp"),
            P(),
        ),
        out_specs=(P(("dp", "mp"), None), P("dp", "mp"), P("mp"), P()),
        check_vma=False,
    )
```

```python
import math

import jax
import jax.numpy as jnp
from jax import lax
from jax.experimental import pallas as pl
from jax.experimental.pallas import tpu as pltpu
from jax.sharding import PartitionSpec as P

SPARSITY = 0.5
D = 4608
LAT = 1024
HALF = D // 2
PART = HALF // 2
ROWS = 16
TOK = 512
BATCH = 256
QROWS = D // 4
SUB = QROWS // 3
OWN = QROWS // 2
TOKENS = 2048
SCALE = 1.0 / math.sqrt(TOKENS)
F32 = jnp.float32
BF16 = jnp.bfloat16
CUTS = (pl.ds(0, PART), pl.ds(PART, PART))
LAST = (((1,), (1,)), ((), ()))
FIRST = (((0,), (0,)), ((), ()))


def kernel(
    attn, oproj, gain, resid, w_hbm, ebias, dbias,
    stream, own_grad, zrecv, enc_out, dec_out,
    w_v, cen, err, cen_y, err_y, pos, lat, pre, lat_y, pre_y,
    rsend, rown, rrecv, p1r2,
    rz, rx, s2a, s2b, r2a, r2b,
    zsend, tmp, res2, str2, att, ssq, gain2, shift2,
    es3, esr, ezr, dcore, dx_r, dz_r, dy_r,
    w_sem, rs_s, rs_r, st_s, st_r, ss_s, ss_r, p1_s, p1_r, p2_s, p2_r, ag_s, ag_r,
    rc_s, rc_r, r1_s, r1_r, r2_s, r2_r,
    yp_s, yp_r, yl_s, yl_r, y_s, y_r, z_s, z_r, b_s, b_r,
):
    dp, mp = lax.axis_index("dp"), lax.axis_index("mp")
    y, zl = dp // 2, dp % 2
    zh, x, c = mp // 8, (mp // 2) % 4, mp % 2
    z = zh * 2 + zl

    def dev(x_, y_, z_, c_):
        return (y_ * 2 + z_ % 2, (z_ // 2) * 8 + x_ * 2 + c_)

    core = dev(x, y, z, 1 - c)

    def xpeer(k):
        return dev((x + k) % 4, y, z, c)

    def zpeer(k):
        return dev(x, y, (z + k) % 4, c)

    def ypeer(k):
        return dev(x, (y + k) % 4, z, c)

    zpart = dev(x, y, zh * 2 + 1 - zl, c)

    def far(j):
        return dev((x + j % 4) % 4, y, ((zh + j // 4) % 2) * 2 + zl, c)

    def remote(src, dst, ssem, rsem, to):
        return pltpu.make_async_remote_copy(
            src_ref=src, dst_ref=dst, send_sem=ssem, recv_sem=rsem,
            device_id=to, device_id_type=pl.DeviceIdType.MESH,
        )

    w_copy = pltpu.make_async_copy(
        w_hbm.at[:, pl.ds(pl.multiple_of(zl * LAT, LAT), LAT)], w_v, w_sem
    )
    w_copy.start()

    barrier = pltpu.get_barrier_semaphore()
    partners = [core]
    for k in (1, 2, 3):
        partners += [xpeer(k), zpeer(k), ypeer(k), far(4 + k)]
    for to in partners:
        pl.semaphore_signal(barrier, inc=1, device_id=to, device_id_type=pl.DeviceIdType.MESH)
    pl.semaphore_wait(barrier, len(partners))

    def half(which, at=0, width=HALF):
        return pl.ds(pl.multiple_of(which * HALF + at, 128), width)

    mine_cols, their_cols = half(c), half(1 - c)

    res_out = remote(resid.at[:, their_cols], res2.at[c], rs_s, rs_r, core)
    res_out.start()
    res2[c] = resid[:, mine_cols]
    row = gain[...].reshape(1, D)
    gain2[...] = jnp.where(c == 0, row[:, :HALF], row[:, HALF:])
    row = dbias[...].reshape(1, D)
    shift2[...] = jnp.where(c == 0, row[:, :HALF], row[:, HALF:])

    def proj(b, which, j):
        rows = attn[:, :, b].reshape(128, 256)
        part = jnp.dot(rows, oproj[:, half(which, j * 768, 768)], preferred_element_type=F32)
        return pl.ds(pl.multiple_of(j * 768, 768), 768), part.reshape(2, 4, ROWS, 768)

    p1, p2 = [], [[], []]
    for b in (0, 1):

        def peer_proj(j, carry, b=b):
            cols, part = proj(b, 1 - c, j)
            rsend[b, pl.ds(0, 2), :, :, cols] = part.astype(BF16)
            return carry

        lax.fori_loop(0, 3, peer_proj, 0)
        two = pl.ds(0, 2)
        p1.append(remote(rsend.at[b, two], rrecv.at[b, two], p1_s.at[b], p1_r.at[b], core))
        p1[b].start()
    for b in (0, 1):

        def own_proj(j, carry, b=b):
            cols, part = proj(b, c, j)
            rown[b, pl.ds(0, 2), :, :, cols] = part
            return carry

        lax.fori_loop(0, 3, own_proj, 0)
        p1[b].wait()

        def add_proj(j, carry, b=b):
            total = rown[b, j // 4, j % 4] + rrecv[b, j // 4, j % 4].astype(F32)
            rown[b, j // 4, j % 4] = total
            rrecv[b, j // 4, j % 4] = total.astype(BF16)
            return carry

        lax.fori_loop(0, 8, add_proj, 0)
        for j in range(1, 8):
            p2[b].append(
                remote(
                    rrecv.at[b, (zh + j // 4) % 2, (x + j % 4) % 4], p1r2.at[b, j - 1],
                    p2_s.at[b, j - 1], p2_r.at[b, j - 1], far(j),
                )
            )
            p2[b][-1].start()

    def gather(at, start, cut, width, phase):
        left = pl.ds(start, cut)
        right = pl.ds(start + cut, width - cut)
        if not isinstance(start, int):
            left = pl.ds(pl.multiple_of(start, 128), cut)
            right = pl.ds(pl.multiple_of(start + cut, 128), width - cut)
        every = slice(None)

        def copy(ref, i, to):
            return remote(ref, ref, ag_s.at[phase, i], ag_r.at[phase, i], to)

        first, second, third = [], [], []
        for k in (1, 2, 3):
            first.append(copy(at(z, x, left), k, xpeer(k)))
            first.append(copy(at(z, x, right), 3 + k, zpeer(k)))
            second.append(copy(at(z, every, left), 6 + k, zpeer(k)))
            second.append(copy(at(every, x, right), 9 + k, xpeer(k)))
        third.append(copy(at(z, every, left), 13, core))
        third.append(copy(at(every, x, right), 14, core))
        for k in (1, 2, 3):
            third.append(copy(at((z + 4 - k) % 4, every, left), 14 + k, core))
            third.append(copy(at(every, (x + 4 - k) % 4, right), 17 + k, core))

        def begin():
            for one in first:
                one.start()

        def spread():
            for one in first:
                one.wait()
            for one in second + third[:2]:
                one.start()

        def share():
            for came, one in zip(second, third[2:]):
                came.wait()
                one.start()

        def end():
            for one in third:
                one.wait()

        return begin, spread, share, end, third

    def rows_of(buf, b, phase):
        return gather(
            lambda z_, x_, cols: buf.at[b, z_, x_, :, cols], c * HALF, PART, HALF, phase
        )

    active = c == y // 2

    def part_of(buf, buf_y, b, phase):
        start, spread, share, end, third = gather(
            lambda z_, x_, cols: buf_y.at[:, b, z_, x_, :, cols], 0, 640, QROWS, 4 + phase
        )

        def piece(k, i):
            to = dev(x, (y + k) % 4, z, c)
            cols = pl.ds(pl.multiple_of(((y + k) % 4) * QROWS, 128), QROWS)
            return remote(
                buf.at[b, z, x, :, cols], buf_y.at[k - 1, b, z, x],
                yp_s.at[phase, i], yp_r.at[phase, k - 1], to,
            )

        def each(act):
            for i in (0, 1):
                k = (2 * c + i + 4 - y) % 4

                @pl.when(k > 0)
                def _(k=k, i=i):
                    act(piece(k, i))

        def send():
            each(lambda copy: copy.start())

        def begin():
            each(lambda copy: copy.wait_send())

            @pl.when(active)
            def _():
                for k in (1, 2, 3):
                    piece(k, 0).wait_recv()
                start()

        def when_active(step):
            def run():
                pl.when(active)(step)

            return run

        def finish():
            @pl.when(active)
            def _():
                for copy in third:
                    copy.wait_send()

            @pl.when(jnp.logical_not(active))
            def _():
                for copy in third:
                    copy.wait_recv()

        return send, begin, when_active(spread), when_active(share), finish

    squares = []

    def sum_squares(b):
        for copy in p2[b]:
            copy.wait()
        total = rown[b, zh, x]
        for j in range(7):
            total = total + p1r2[b, j].astype(F32)
        att[b] = total
        own_sq = jnp.sum(total * total, axis=-1, keepdims=True)
        ssq[b, c] = jnp.broadcast_to(own_sq, (ROWS, 128))
        mine = ssq.at[b, c]
        squares.append(remote(mine, mine, ss_s.at[b], ss_r.at[b], core))
        squares[b].start()

    def norm(b):
        squares[b].wait()
        mean_sq = (ssq[b, 0] + ssq[b, 1])[:, 0:1] * (1.0 / D)
        normed = att[b] * lax.rsqrt(mean_sq + 1e-06) * gain2[...]
        rows = (res2[b].astype(F32) + normed).astype(BF16)
        str2[b] = rows
        cen[b, z, x, :, mine_cols] = (rows.astype(F32) - shift2[...]).astype(BF16)

    cen_rows = [rows_of(cen, b, b) for b in (0, 1)]
    err_rows = [rows_of(err, b, 2 + b) for b in (0, 1)]
    cen_part = [part_of(cen, cen_y, b, b) for b in (0, 1)]
    err_part = [part_of(err, err_y, b, 2 + b) for b in (0, 1)]

    sum_squares(0)
    res_out.wait()
    norm(0)
    cen_rows[0][0]()
    cen_part[0][0]()
    sum_squares(1)
    norm(1)
    cen_rows[1][0]()
    cen_part[1][0]()
    stream_out = remote(str2.at[1 - c], stream.at[:, mine_cols], st_s, st_r, core)
    stream_out.start()
    stream[:, mine_cols] = str2[c]

    cen_rows[0][1]()
    cen_rows[1][1]()
    cen_part[0][1]()
    cen_part[1][1]()
    row = ebias[...].reshape(2, LAT)
    ezr[0:1, :] = jnp.where(zl == 0, row[0:1], row[1:2])
    w_copy.wait()

    def encode(b):
        def body(n, carry):
            cols = pl.ds(pl.multiple_of(n * 256, 256), 256)
            act = jnp.dot(
                cen[b].reshape(BATCH, D), w_v[:, cols], preferred_element_type=F32
            )
            act = jnp.maximum(act + ezr[0:1, cols], 0.0)
            pos[b, :, cols] = act
            lat[b, :, cols] = (act * act).astype(BF16)
            return carry

        lax.fori_loop(0, 4, body, 0)

    def round_y(own, got, cols, s_sem, r_sem):
        top, low = pl.ds(0, BATCH // 2), pl.ds(BATCH // 2, BATCH // 2)
        near = [
            remote(own.at[:, cols], got(0).at[:, cols], s_sem.at[0], r_sem.at[0], ypeer(1)),
            remote(own.at[:, cols], got(2).at[:, cols], s_sem.at[1], r_sem.at[1], ypeer(3)),
        ]
        on = [
            remote(
                got(0).at[top, cols], got(1).at[top, cols], s_sem.at[2], r_sem.at[2], ypeer(1)
            ),
            remote(
                got(2).at[low, cols], got(1).at[low, cols], s_sem.at[3], r_sem.at[3], ypeer(3)
            ),
        ]

        def begin():
            for copy in near:
                copy.start()

        def onward():
            for copy, came in zip(on, near):
                came.wait()
                copy.start()

        def end():
            for copy in on:
                copy.wait()

        return begin, onward, end

    lat_round = [
        round_y(
            lat.at[b], lambda k, b=b: lat_y.at[k, b], pl.ds(0, LAT), yl_s.at[b], yl_r.at[b]
        )
        for b in (0, 1)
    ]

    def decode(b, which, j):
        rows = half(which, j * 256, 256)
        part = lax.dot_general(lat[b], w_v[rows, :], LAST, preferred_element_type=F32)
        return pl.ds(pl.multiple_of(j * 256, 256), 256), part.reshape(4, 4, ROWS, 256)

    rc, r1, r2 = [], [[], []], [[], []]

    def decode_peer(b):
        def body(j, carry):
            cols, part = decode(b, 1 - c, j)
            rsend[b, :, :, :, cols] = part.astype(BF16)
            return carry

        lax.fori_loop(0, 9, body, 0)
        rc.append(remote(rsend.at[b], rrecv.at[b], rc_s.at[b], rc_r.at[b], core))
        rc[b].start()

    def decode_own(b):
        def body(j, carry):
            cols, part = decode(b, c, j)
            rown[b, :, :, :, cols] = part
            return carry

        lax.fori_loop(0, 9, body, 0)

    def recon_first(b):
        rc[b].wait()

        def body(j, carry):
            total = rown[b, j // 4, j % 4] + rrecv[b, j // 4, j % 4].astype(F32)
            rown[b, j // 4, j % 4] = total
            rrecv[b, j // 4, j % 4] = total.astype(BF16)
            return carry

        lax.fori_loop(0, 16, body, 0)
        for k in (1, 2, 3):
            for h in (0, 1):
                if h == 0:
                    src, dst, to = rrecv.at[b, (z + k) % 4, :, :, CUTS[0]], rz, zpeer(k)
                else:
                    src, dst, to = rrecv.at[b, :, (x + k) % 4, :, CUTS[1]], rx, xpeer(k)
                i = 2 * k - 2 + h
                r1[b].append(remote(src, dst.at[b, k - 1], r1_s.at[b, i], r1_r.at[b, i], to))
                r1[b][-1].start()

    def recon_second(b):
        for copy in r1[b]:
            copy.wait()
        for i in range(4):
            total = rown[b, z, i, :, CUTS[0]]
            for k in range(3):
                total = total + rz[b, k, i].astype(F32)
            rown[b, z, i, :, CUTS[0]] = total
            s2a[b, i] = total.astype(BF16)
            total = rown[b, i, x, :, CUTS[1]]
            for k in range(3):
                total = total + rx[b, k, i].astype(F32)
            rown[b, i, x, :, CUTS[1]] = total
            s2b[b, i] = total.astype(BF16)
        for k in (1, 2, 3):
            for h in (0, 1):
                if h == 0:
                    src, dst, to = s2a.at[b, (x + k) % 4], r2a, xpeer(k)
                else:
                    src, dst, to = s2b.at[b, (z + k) % 4], r2b, zpeer(k)
                i = 2 * k - 2 + h
                r2[b].append(remote(src, dst.at[b, k - 1], r2_s.at[b, i], r2_r.at[b, i], to))
                r2[b][-1].start()

    def error(b):
        for copy in r2[b]:
            copy.wait()
        for h in (0, 1):
            total = rown[b, z, x, :, CUTS[h]]
            for k in range(3):
                total = total + (r2a, r2b)[h][b, k].astype(F32)
            grad = total + shift2[:, CUTS[h]] - str2[b, :, CUTS[h]].astype(F32)
            grad = (grad * SCALE).astype(BF16)
            cols = half(c, h * PART, PART)
            err[b, z, x, :, cols] = grad
            sums = jnp.sum(grad.astype(F32), axis=0, keepdims=True)
            dcore[pl.ds(c, 1), cols] = dcore[pl.ds(c, 1), cols] + sums

    cen_rows[0][2]()
    cen_rows[0][3]()
    encode(0)
    lat_round[0][0]()
    cen_part[0][2]()
    decode_peer(0)
    decode_own(0)
    cen_rows[1][2]()
    recon_first(0)
    cen_rows[1][3]()
    encode(1)
    lat_round[1][0]()
    cen_part[1][2]()
    decode_peer(1)
    decode_own(1)
    recon_first(1)
    lat_round[0][1]()
    dcore[pl.ds(c, 1), :] = jnp.zeros((1, D), F32)
    recon_second(0)
    recon_second(1)
    cen_part[0][3]()
    error(0)
    err_rows[0][0]()
    err_part[0][0]()
    error(1)
    err_rows[1][0]()
    err_part[1][0]()
    err_rows[0][1]()
    err_rows[1][1]()
    cen_part[1][3]()
    lat_round[1][1]()
    err_part[0][1]()
    err_part[1][1]()
    err_rows[0][2]()
    err_rows[0][3]()

    def back(b):
        def body(n, carry):
            cols = pl.ds(pl.multiple_of(n * 256, 256), 256)
            grad = jnp.dot(
                err[b].reshape(BATCH, D), w_v[:, cols], preferred_element_type=F32
            )
            grad = ((grad + SPARSITY * SCALE) * (2.0 * pos[b, :, cols])).astype(BF16)
            pre[b, n] = grad
            sums = jnp.sum(grad.astype(F32), axis=0, keepdims=True)
            if b == 1:
                sums = sums + esr[pl.ds(y, 1), cols]
            esr[pl.ds(y, 1), cols] = sums
            return carry

        lax.fori_loop(0, 4, body, 0)

    pre_round = [
        [
            round_y(
                pre.at[b, n], lambda k, b=b, n=n: pre_y.at[k, b, n], pl.ds(0, 256),
                y_s.at[b, n], y_r.at[b, n],
            )
            for n in range(4)
        ]
        for b in (0, 1)
    ]
    back(0)
    pre_round[0][0][0]()
    pre_round[0][1][0]()
    err_part[0][2]()
    err_rows[1][2]()
    err_rows[1][3]()
    back(1)
    pre_round[1][0][0]()
    pre_round[1][1][0]()
    err_part[1][2]()
    pre_round[0][0][1]()
    pre_round[0][1][1]()

    own_sum = esr[pl.ds(y, 1), :]
    high = own_sum.astype(BF16)
    rest = own_sum - high.astype(F32)
    mid = rest.astype(BF16)
    bottom = (rest - mid.astype(F32)).astype(BF16)
    es3[...] = jnp.concatenate([high, mid, bottom, jnp.zeros((13, LAT), BF16)], axis=0)

    def b_copy(src, dst, i, to):
        return remote(src, dst, b_s.at[i], b_r.at[i], to)

    bias = []
    mine = esr.at[pl.ds(y, 1)]
    for k in (1, 2, 3):
        bias.append(b_copy(mine, mine, k - 1, ypeer(k)))
    for copy in bias:
        copy.start()

    def project(j, carry):
        cols = pl.ds(pl.multiple_of(j * 512, 512), 512)
        part = lax.dot_general(es3[...], w_v[cols, :], LAST, preferred_element_type=F32)
        dcore[pl.ds(c, 1), cols] = dcore[pl.ds(c, 1), cols] - jnp.sum(part, axis=0, keepdims=True)
        return carry

    def dec_stage(slots, value, me, first, peer):
        slots[pl.ds(me, 1), :] = value
        mine = slots.at[pl.ds(me, 1)]
        out = [b_copy(mine, mine, first + k, peer(k + 1)) for k in range(3)]
        for copy in out:
            copy.start()
        return out

    def ordered(slots, count):
        total = slots[0:1, :]
        for i in range(1, count):
            total = total + slots[i : i + 1, :]
        return total

    def grad_chunk(n):
        cols = pl.ds(n * 256, 256)

        def body(sub, carry):
            at = pl.ds(pl.multiple_of(sub * SUB, 128), SUB)
            own_at = pl.ds(pl.multiple_of(y * QROWS + sub * SUB, 128), SUB)

            def outer(rows, values):
                return lax.dot_general(
                    rows.reshape(TOK, SUB), values.reshape(TOK, 256), FIRST,
                    preferred_element_type=F32,
                )

            total = outer(cen[:, :, :, :, own_at], pre[:, n])
            total = total + outer(err[:, :, :, :, own_at], lat[:, :, cols])
            for k in range(3):
                total = total + outer(cen_y[k, :, :, :, :, at], pre_y[k, :, n])
                total = total + outer(err_y[k, :, :, :, :, at], lat_y[k, :, :, cols])
            tmp[pl.ds(pl.multiple_of(sub * SUB, 128), SUB), :] = total
            return carry

        lax.fori_loop(0, 3, body, 0)
        theirs = pl.ds(pl.multiple_of((1 - zl) * OWN, 64), OWN)
        ours = pl.ds(pl.multiple_of(zl * OWN, 64), OWN)
        zsend[n] = tmp[theirs, :].astype(BF16)
        copy = remote(zsend.at[n], zrecv.at[n], z_s.at[n], z_r.at[n], zpart)
        copy.start()
        own_grad[:, cols] = tmp[ours, :]
        return copy

    pre_round[1][0][1]()
    pre_round[0][2][0]()
    pre_round[1][2][0]()
    err_part[0][3]()
    pre_round[1][1][1]()
    pre_round[0][3][0]()
    pre_round[1][3][0]()
    err_part[1][3]()
    for b in (0, 1):
        cen_part[b][4]()
        lat_round[b][2]()
        err_part[b][4]()

    zout = []
    for n in range(4):
        for b in (0, 1):
            pre_round[b][n][2]()
        zout.append(grad_chunk(n))
        if n < 2:
            for b in (0, 1):
                pre_round[b][n + 2][1]()
        for copy in bias:
            copy.wait()
        if n == 0:
            ezr[pl.ds(zl, 1), :] = ordered(esr, 4)
            mine = ezr.at[pl.ds(zl, 1)]
            enc = b_copy(mine, mine, 4, zpart)
            enc.start()
            lax.fori_loop(0, 9, project, 0)
            mine = dcore.at[pl.ds(c, 1)]
            bias = [b_copy(mine, mine, 3, core)]
            bias[0].start()
        elif n == 1:
            bias = dec_stage(dx_r, ordered(dcore, 2), x, 5, xpeer)
        elif n == 2:
            bias = dec_stage(dz_r, ordered(dx_r, 4), z, 8, zpeer)
        else:
            bias = dec_stage(dy_r, ordered(dz_r, 4), y, 11, ypeer)
    stream_out.wait()
    enc.wait()
    enc_out[...] = ezr[...]
    for copy in bias:
        copy.wait()
    dec_out[...] = ordered(dy_r, 4)
    for copy in zout:
        copy.wait()


def write_out(stream, own_grad, their_grad, enc, dec, stream_out, wgrad, enc_out, dec_out):
    zl = lax.axis_index("dp") % 2
    here = pl.ds(pl.multiple_of(zl * LAT, LAT), LAT)
    wgrad[:, here] = own_grad[...]
    for n in range(4):
        there = pl.ds(pl.multiple_of((1 - zl) * LAT + n * 256, 256), 256)
        wgrad[:, there] = their_grad[n].astype(F32)

    @pl.when(pl.program_id(0) == 0)
    def _():
        stream_out[...] = stream[...]
        enc_out[pl.ds(0, LAT)] = enc[0, :]
        enc_out[pl.ds(LAT, LAT)] = enc[1, :]
        dec_out[...] = dec[0, :]


def per_device(attn_values, out_proj, post_gain, residual, sae_weight, enc_bias, dec_bias):
    vmem = pl.BlockSpec(memory_space=pltpu.VMEM)
    hbm = pl.BlockSpec(memory_space=pl.ANY)
    block = (2, 4, 4, ROWS, HALF)
    dma = pltpu.SemaphoreType.DMA
    parts = pl.pallas_call(
        kernel,
        out_shape=(
            jax.ShapeDtypeStruct((ROWS, D), BF16),
            jax.ShapeDtypeStruct((OWN, LAT), F32),
            jax.ShapeDtypeStruct((4, OWN, 256), BF16),
            jax.ShapeDtypeStruct((2, LAT), F32),
            jax.ShapeDtypeStruct((1, D), F32),
        ),
        in_specs=[vmem, vmem, vmem, vmem, hbm, vmem, vmem],
        out_specs=(vmem, vmem, vmem, vmem, vmem),
        scratch_shapes=[
            pltpu.VMEM((D, LAT), BF16),
            pltpu.VMEM((2, 4, 4, ROWS, D), BF16),
            pltpu.VMEM((2, 4, 4, ROWS, D), BF16),
            pltpu.VMEM((3, 2, 4, 4, ROWS, QROWS), BF16),
            pltpu.VMEM((3, 2, 4, 4, ROWS, QROWS), BF16),
            pltpu.VMEM((2, BATCH, LAT), F32),
            pltpu.VMEM((2, BATCH, LAT), BF16),
            pltpu.VMEM((2, 4, BATCH, 256), BF16),
            pltpu.VMEM((3, 2, BATCH, LAT), BF16),
            pltpu.VMEM((3, 2, 4, BATCH, 256), BF16),
            pltpu.VMEM(block, BF16),
            pltpu.VMEM(block, F32),
            pltpu.VMEM(block, BF16),
            pltpu.VMEM((2, 7, ROWS, HALF), BF16),
            pltpu.VMEM((2, 3, 4, ROWS, PART), BF16),
            pltpu.VMEM((2, 3, 4, ROWS, PART), BF16),
            pltpu.VMEM((2, 4, ROWS, PART), BF16),
            pltpu.VMEM((2, 4, ROWS, PART), BF16),
            pltpu.VMEM((2, 3, ROWS, PART), BF16),
            pltpu.VMEM((2, 3, ROWS, PART), BF16),
            pltpu.VMEM((4, OWN, 256), BF16),
            pltpu.VMEM((QROWS, 256), F32),
            pltpu.VMEM((2, ROWS, HALF), BF16),
            pltpu.VMEM((2, ROWS, HALF), BF16),
            pltpu.VMEM((2, ROWS, HALF), F32),
            pltpu.VMEM((2, 2, ROWS, 128), F32),
            pltpu.VMEM((1, HALF), F32),
            pltpu.VMEM((1, HALF), F32),
            pltpu.VMEM((16, LAT), BF16),
            pltpu.VMEM((4, LAT), F32),
            pltpu.VMEM((2, LAT), F32),
            pltpu.VMEM((2, D), F32),
            pltpu.VMEM((4, D), F32),
            pltpu.VMEM((4, D), F32),
            pltpu.VMEM((4, D), F32),
            dma, dma, dma, dma, dma, dma((2,)), dma((2,)), dma((2,)), dma((2,)),
            dma((2, 7)), dma((2, 7)), dma((8, 21)), dma((8, 21)),
            dma((2,)), dma((2,)), dma((2, 6)), dma((2, 6)), dma((2, 6)), dma((2, 6)),
            dma((4, 2)), dma((4, 3)), dma((2, 4)), dma((2, 4)), dma((2, 4, 4)), dma((2, 4, 4)),
            dma((4,)), dma((4,)), dma((14,)), dma((14,)),
        ],
        compiler_params=pltpu.CompilerParams(
            collective_id=0, has_side_effects=True, vmem_limit_bytes=63 * 2**20
        ),
        cost_estimate=pl.CostEstimate(
            flops=25 * 10**9, bytes_accessed=20 * 10**6, transcendentals=0
        ),
    )(
        attn_values.reshape(2, 4, 2, ROWS, 256),
        out_proj, post_gain, residual, sae_weight, enc_bias, dec_bias,
    )
    steps = 3

    def fixed(*shape):
        return pl.BlockSpec(shape, lambda i: (0,) * len(shape))

    def rows(width):
        return pl.BlockSpec((OWN // steps, width), lambda i: (i, 0))

    return tuple(
        pl.pallas_call(
            write_out,
            grid=(steps,),
            out_shape=(
                jax.ShapeDtypeStruct((ROWS, D), BF16),
                jax.ShapeDtypeStruct((OWN, 2 * LAT), F32),
                jax.ShapeDtypeStruct((2 * LAT,), F32),
                jax.ShapeDtypeStruct((D,), F32),
            ),
            in_specs=[
                fixed(ROWS, D),
                rows(LAT),
                pl.BlockSpec((4, OWN // steps, 256), lambda i: (0, i, 0)),
                fixed(2, LAT),
                fixed(1, D),
            ],
            out_specs=(fixed(ROWS, D), rows(2 * LAT), fixed(2 * LAT), fixed(D)),
        )(*parts)
    )


def solution(mesh):
    return jax.shard_map(
        per_device,
        mesh=mesh,
        in_specs=(
            P("dp", "mp"),
            P("mp", None),
            P(),
            P(("dp", "mp"), None),
            P(None, "mp"),
            P("mp"),
            P(),
        ),
        out_specs=(P(("dp", "mp"), None), P("dp", "mp"), P("mp"), P()),
        check_vma=False,
    )
```
